512 devices in a mesh: dp: 16 (over y, core), item: 32 (over x, z).
Axes of the slice: x: 4, y: 8, z: 8, core: 2. Of those that a mesh axis runs over, the one named last changes fastest.
Arguments:
- query: bfloat16 [512, 256], P(('dp', 'item')), may hold values from -40 to 40
- item_table: bfloat16 [1048576, 256], P(('dp', 'item')), may hold values from -2.5 to 2.5
- context_features: bfloat16 [512, 512], P(('dp', 'item')), may hold values from -6 to 6
- candidates: int32 [512, 1024], P(('dp', 'item')), may hold values from 0 to 1048575, as said below
- lengths: int32 [512], P(('dp', 'item')), may hold values from 128 to 1024, as said below
- logged_slot: int32 [512], P(('dp', 'item')), may hold values from 0 to 1023, as said below
- logging_prop: int32 [512], P(('dp', 'item')), may hold values from 256 to 4095
- w_first: bfloat16 [768, 512], replicated, may hold values from -0.21875 to 0.21875
- w_second: bfloat16 [512, 512], replicated, may hold values from -0.25 to 0.25
- w_score: bfloat16 [512], replicated, may hold values from -0.5 to 0.5
Outputs:
- section_logp: float32 [512, 1024], P(('dp', 'item'))
- log_weight: float32 [512], P(('dp', 'item'))
The draws below stay inside these ranges and needn't reach their ends.
Inputs may be any that keep to these rules, and one draw needn't show every extreme that they name: `candidates`: item ids. Among the 1024 candidate slots held by one device (its single context), at most 3 name items of any one block of 2048 consecutive ids, and for every device some block is named exactly 3 times. `lengths`: some context's list has 1024 live slots and some context's list has 128. `logged_slot`: below the context's length; the context with the longest list logs its last slot.
All inputs are finite; a program needn't handle non-finite values.
Results may differ from the reference program's by a relative error of at most 0.0003.
Values may be sent and summed in bfloat16 or wider, within the bound.
No kernel may reach another device: no remote copies, remote signals or barrier semaphores. Data moves between devices by JAX's collectives and lax.ppermute only.
A program may use at most 64 MiB of HBM per device.

```python
import math
import jax
import jax.numpy as jnp
from jax import lax

D = 256
CF = 512
H = 512
ITEM_DEV = 2048
CTX_DEV = 1
CAND_MAX = 1024
MIN_LEN = 128
CTX = 512
ITEMS = 1048576
CAP = 3
DEVICES = 512


def table_row(base_key, index):
    row_key = jax.random.fold_in(base_key, index)
    raw = jax.random.truncated_normal(row_key, -6.0, 6.0, (D,), jnp.float32)
    level = jax.random.uniform(jax.random.fold_in(row_key, 7), (), jnp.float32, 0.0, 1.0)
    spread = jnp.exp(level * jnp.log(jnp.float32(3.0))) * 2.0 / jnp.sqrt(jnp.float32(D))
    return jnp.clip(raw * spread, -2.5, 2.5)


def draw_item_table(key, part):
    base_key = jax.random.fold_in(key, 101)
    indices = jnp.arange(ITEMS, dtype=jnp.int32)
    rows = jax.vmap(lambda index: table_row(base_key, index))(indices)
    return rows.astype(jnp.bfloat16)


def draw_query(key, part):
    entries = jax.random.truncated_normal(jax.random.fold_in(key, 202), -6.0, 6.0, (CTX, D), jnp.float32)
    return entries.astype(jnp.bfloat16)


def draw_candidates(key, part):
    block_count = CTX // CTX_DEV
    slot_count = CTX_DEV * CAND_MAX

    def one_block(block_key):
        keys = jax.random.split(block_key, 4)
        leader = jax.random.randint(keys[0], (), 0, block_count)
        others = CAP + jax.random.permutation(keys[1], block_count * CAP - CAP)[:slot_count - CAP]
        picked = jnp.concatenate([jnp.arange(CAP, dtype=jnp.int32), others.astype(jnp.int32)])
        holder = (leader + picked // CAP) % block_count
        holder = holder[jax.random.permutation(keys[2], slot_count)]
        inside = jax.random.randint(keys[3], (slot_count,), 0, ITEM_DEV)
        return (holder * ITEM_DEV + inside).reshape(CTX_DEV, CAND_MAX)
    keys = jax.random.split(jax.random.fold_in(key, 303), block_count)
    return jax.vmap(one_block)(keys).reshape(CTX, CAND_MAX).astype(jnp.int32)


def longest_index(key):
    keys = jax.random.split(jax.random.fold_in(key, 404), 2)
    return jax.random.randint(keys[1], (), 0, CTX)


def list_lengths(key):
    keys = jax.random.split(jax.random.fold_in(key, 404), 1)
    drawn = jax.random.randint(keys[0], (CTX,), MIN_LEN, CAND_MAX + 1)
    longest = longest_index(key)
    shortest = (longest + 1) % CTX
    drawn = drawn.at[shortest].set(MIN_LEN)
    return drawn.at[longest].set(CAND_MAX).astype(jnp.int32)


def draw_lengths(key, part):
    return list_lengths(key)


def draw_logged_slot(key, part):
    list_len = list_lengths(key)
    drawn = jax.random.randint(jax.random.fold_in(key, 505), (CTX,), 0, 1 << 20)
    slots = drawn % list_len
    longest = longest_index(key)
    shortest = (longest + 1) % CTX
    slots = slots.at[shortest].set(0)
    slots = slots.at[longest].set(CAND_MAX - 1)
    return slots.astype(jnp.int32)


def touch_ends(result, own_key, smallest, largest):
    extent = result.shape
    spot = [jax.random.randint(jax.random.fold_in(own_key, axis), (), 0, extent[axis]) for axis in range(len(extent))]
    result = result.at[tuple(spot)].set(smallest)
    longest = extent.index(max(extent))
    spot[longest] = (spot[longest] + 1) % extent[longest]
    return result.at[tuple(spot)].set(largest)


def shard_levels(rng, shape, cuts, low, high):
    level, own = 1.0, jax.random.fold_in(rng, 6)
    for position, blocks in cuts:
        steps = jnp.exp(jax.random.uniform(jax.random.fold_in(own, position), (blocks,), jnp.float32, low / len(cuts), high / len(cuts)))
        level = level * jnp.repeat(steps, shape[position] // blocks).reshape([-1 if axis == position else 1 for axis in range(len(shape))])
    return level


def centred(stream_key, shape, deviation, bound, pieces=(), kind=jnp.bfloat16):
    values = jax.random.normal(stream_key, shape, jnp.float32) * deviation
    if len(pieces) > 0:
        values = shard_levels(stream_key, shape, pieces, -0.22, 0.18) * values
    return jnp.clip(values, min=-bound, max=bound).astype(kind)


def setup_inputs(seed: int = 0) -> dict:
    streams_of = jax.random.split(jax.random.key(seed), 11)
    query = draw_query(jax.random.fold_in(streams_of[10], 71), 0)
    item_table = draw_item_table(jax.random.fold_in(streams_of[10], 71), 0)
    context_features = centred(streams_of[2], (CTX, CF), 1.0, 6.0, ((0, 512),))
    candidates = draw_candidates(jax.random.fold_in(streams_of[10], 71), 0)
    lengths = draw_lengths(jax.random.fold_in(streams_of[10], 71), 0)
    logged_slot = draw_logged_slot(jax.random.fold_in(streams_of[10], 71), 0)
    logging_prop = touch_ends(jax.random.randint(streams_of[6], (CTX,), 256, 4096), jax.random.fold_in(streams_of[6], 1), 256, 4095).astype(jnp.int32)
    w_first = centred(streams_of[7], (CF + D, H), (CF + D) ** -0.5, 0.21875)
    w_second = centred(streams_of[8], (H, H), H ** -0.5, 0.25)
    w_score = centred(streams_of[9], (H,), 128 ** -0.5, 0.5)
    return {"query": query, "item_table": item_table, "context_features": context_features, "candidates": candidates, "lengths": lengths, "logged_slot": logged_slot, "logging_prop": logging_prop, "w_first": w_first, "w_second": w_second, "w_score": w_score}


def reference(query, item_table, context_features, candidates, lengths, logged_slot, logging_prop, w_first, w_second, w_score):
    slabs = item_table.reshape(DEVICES, ITEM_DEV, D)

    def sweep(running, slab_rows):
        running_max, running_sum = running
        logits = jnp.dot(query, slab_rows.T, preferred_element_type=jnp.float32)
        new_max = jnp.maximum(running_max, jnp.max(logits, axis=1))
        new_sum = running_sum * jnp.exp(running_max - new_max) + jnp.sum(jnp.exp(logits - new_max[:, None]), axis=1)
        return (new_max, new_sum), None

    initial = (jnp.full((CTX,), -1e30, jnp.float32), jnp.zeros((CTX,), jnp.float32))
    (running_max, running_sum), unused_out = lax.scan(sweep, initial, slabs)
    log_norm = running_max + jnp.log(running_sum)
    positions = jnp.arange(CAND_MAX, dtype=jnp.int32)

    def per_context(packed):
        query_row, feature_row, item_ids, list_length, norm_value, logged_index, propensity = packed
        cand_rows = item_table[item_ids]
        gen_logit = jnp.dot(cand_rows, query_row, preferred_element_type=jnp.float32)
        context_part = jnp.dot(feature_row[None, :], w_first[:CF], preferred_element_type=jnp.float32)
        item_part = jnp.dot(cand_rows, w_first[CF:], preferred_element_type=jnp.float32)
        hidden = jax.nn.silu(item_part + context_part).astype(jnp.bfloat16)
        second = jax.nn.silu(jnp.dot(hidden, w_second, preferred_element_type=jnp.float32)).astype(jnp.bfloat16)
        score = jnp.dot(second, w_score, preferred_element_type=jnp.float32)
        live_slots = positions < list_length
        masked = jnp.where(live_slots, score, jnp.float32(-1e30))
        rank_peak = jnp.max(masked)
        rank_norm = rank_peak + jnp.log(jnp.sum(jnp.where(live_slots, jnp.exp(masked - rank_peak), jnp.float32(0.0))))
        section = jnp.where(live_slots, score - rank_norm + gen_logit - norm_value + math.log(ITEMS), jnp.float32(0.0))
        chosen = jnp.sum(jnp.where(positions == logged_index, section, jnp.float32(0.0)))
        weight = chosen + jnp.log(list_length.astype(jnp.float32)) - jnp.log(propensity.astype(jnp.float32) / 1024.0)
        return section, weight

    section_logp, log_weight = lax.map(per_context, (query, context_features, candidates, lengths, log_norm, logged_slot, logging_prop))
    return section_logp, log_weight
```

```python
import math

import jax
import jax.numpy as jnp
from jax import lax
from jax.experimental import pallas as pl
from jax.experimental.pallas import tpu as pltpu
from jax.sharding import Mesh
from jax.sharding import PartitionSpec as P

ALL = ("y", "core", "x", "z")
CHIPS = ("y", "x", "z")
BIG = 1 << 24
CAP = 3
BF = jnp.bfloat16
F32 = jnp.float32


def dot_nt(a, b):
    return lax.dot_general(a, b, (((1,), (1,)), ((), ())), preferred_element_type=F32)


def dot_nn(a, b):
    return lax.dot_general(a, b, (((1,), (0,)), ((), ())), preferred_element_type=F32)


def silu(v):
    half = 0.5 * v
    return half + half * jnp.tanh(half)


def ask_kernel(plane, chips, item_rows, query_ref, feature_ref, ids_ref, payload_ref, pick_ref):
    slots = ids_ref.shape[1]
    ids = ids_ref[...]
    holder = ids // item_rows
    local = ids % item_rows
    slot = lax.broadcasted_iota(jnp.int32, ids.shape, 1)
    key = slot * item_rows + local
    chip = lax.broadcasted_iota(jnp.int32, (chips, 1), 0)
    lane = lax.broadcasted_iota(jnp.int32, (chips, 256), 1)
    asked = jnp.zeros((chips, 256), F32)
    first = jnp.zeros((1, slots), jnp.int32)
    last = jnp.zeros((1, slots), jnp.int32)
    for core in range(2):
        device = (chip // plane) * (2 * plane) + core * plane + chip % plane
        mine = holder == device
        low = jnp.min(jnp.where(mine, key, BIG), axis=1, keepdims=True)
        high = jnp.max(jnp.where(mine, key, -1), axis=1, keepdims=True)
        total = jnp.sum(jnp.where(mine, key, 0), axis=1, keepdims=True)
        middle = total - low - high
        have = (high >= 0, (high > low) & (middle > 0), high > low)
        for j, (wanted, ok) in enumerate(zip((low, middle, high), have)):
            inside = jnp.where(ok, wanted % item_rows, 2 * item_rows)
            place = 2 * (core * CAP + j)
            asked = jnp.where(lane == place, (inside // 256).astype(F32), asked)
            asked = jnp.where(lane == place + 1, (inside % 256).astype(F32), asked)
        first = first + jnp.sum(jnp.where(low == key, 1, 0), axis=0, keepdims=True)
        last = last + jnp.sum(jnp.where(high == key, 1, 0), axis=0, keepdims=True)
    width = query_ref.shape[1]
    feature_width = feature_ref.shape[1]
    payload_ref[:, :width] = jnp.broadcast_to(query_ref[...], (chips, width))
    payload_ref[:, width : width + feature_width] = jnp.broadcast_to(
        feature_ref[...], (chips, feature_width)
    )
    payload_ref[:, width + feature_width :] = asked.astype(BF)
    place = jnp.where(first > 0, 0, jnp.where(last > 0, 2, 1))
    pick_ref[...] = ((holder // plane) % 2) * CAP + place


def hold_kernel(asked_ref, table_ref, w_first_ref, w_second_ref, w_score_ref, out_ref, logits_ref):
    contexts = asked_ref.shape[0]
    width = table_ref.shape[2]
    item_rows = table_ref.shape[1]
    feature_width = w_first_ref.shape[0] - width
    query = asked_ref[:, :width]
    lane = lax.broadcasted_iota(jnp.int32, (contexts, 128), 1)
    chunk = 512
    peak = jnp.full((contexts, 128), -1e30, F32)
    for core in range(2):
        for start in range(0, item_rows, chunk):
            logits = dot_nt(query, table_ref[core, start : start + chunk, :])
            at = core * item_rows + start
            logits_ref[:, at : at + chunk] = logits
            for k in range(0, chunk, 128):
                peak = jnp.maximum(peak, logits[:, k : k + 128])
    peak = jnp.max(peak, axis=1, keepdims=True)
    total = jnp.zeros((contexts, 128), F32)
    for start in range(0, 2 * item_rows, 128):
        total = total + jnp.exp(logits_ref[:, start : start + 128] - peak)
    total = jnp.sum(total, axis=1, keepdims=True)
    out = jnp.where(lane == 4 * CAP, peak, jnp.where(lane == 4 * CAP + 1, total, 0.0))

    context_part = dot_nn(
        asked_ref[:, width : width + feature_width], w_first_ref[:feature_width, :]
    )
    query_wide = query.astype(F32)
    id_parts = asked_ref[:, width + feature_width :].astype(F32)
    item = lax.broadcasted_iota(jnp.int32, (contexts, item_rows), 1)
    w_score = jnp.broadcast_to(w_score_ref[...], (128, w_score_ref.shape[1]))
    for core in range(2):
        for j in range(CAP):
            place = core * CAP + j
            inside = id_parts[:, 2 * place : 2 * place + 1] * 256.0
            inside = (inside + id_parts[:, 2 * place + 1 : 2 * place + 2]).astype(jnp.int32)
            chosen = jnp.where(item == inside, 1.0, 0.0).astype(BF)
            rows = dot_nn(chosen, table_ref[core])
            gen = jnp.sum(rows * query_wide, axis=1, keepdims=True)
            hidden = silu(dot_nn(rows.astype(BF), w_first_ref[feature_width:, :]) + context_part)
            second = silu(dot_nn(hidden.astype(BF), w_second_ref[...]))
            score = dot_nt(second.astype(BF), w_score)
            out = jnp.where(lane == place, score, out)
            out = jnp.where(lane == 2 * CAP + place, gen, out)
    out_ref[...] = out


def own_kernel(
    plane, item_rows, total_items,
    back_ref, ids_ref, pick_ref, length_ref, logged_ref, prop_ref, section_ref, weight_ref,
):
    chips = back_ref.shape[0]
    slots = ids_ref.shape[1]
    back = jnp.transpose(back_ref[...])[:16]
    peaks, sums = back[4 * CAP : 4 * CAP + 1], back[4 * CAP + 1 : 4 * CAP + 2]
    peak = jnp.max(peaks, axis=1, keepdims=True)
    log_norm = peak + jnp.log(jnp.sum(sums * jnp.exp(peaks - peak), axis=1, keepdims=True))
    holder = ids_ref[...] // item_rows
    chip_of = (holder // (2 * plane)) * plane + holder % plane
    chip = lax.broadcasted_iota(jnp.int32, (chips, slots), 0)
    chosen = jnp.where(chip == chip_of, 1.0, 0.0).astype(BF)
    top = back.astype(BF)
    rest = back - top.astype(F32)
    middle = rest.astype(BF)
    low = (rest - middle.astype(F32)).astype(BF)
    found = dot_nn(top, chosen) + dot_nn(middle, chosen) + dot_nn(low, chosen)
    pick = pick_ref[...]
    score = jnp.zeros((1, slots), F32)
    gen = jnp.zeros((1, slots), F32)
    for place in range(2 * CAP):
        score = jnp.where(pick == place, found[place : place + 1], score)
        gen = jnp.where(pick == place, found[2 * CAP + place : 2 * CAP + place + 1], gen)
    slot = lax.broadcasted_iota(jnp.int32, (1, slots), 1)
    length = length_ref[0]
    live = slot < length
    masked = jnp.where(live, score, -1e30)
    rank_peak = jnp.max(masked, axis=1, keepdims=True)
    rank_sum = jnp.sum(jnp.where(live, jnp.exp(masked - rank_peak), 0.0), axis=1, keepdims=True)
    rank_norm = rank_peak + jnp.log(rank_sum)
    section = jnp.where(live, score - rank_norm + gen - log_norm + math.log(total_items), 0.0)
    section_ref[...] = section
    chosen = jnp.sum(jnp.where(slot == logged_ref[0], section, 0.0), axis=1, keepdims=True)
    ones = jnp.ones((1, 128), F32)
    weight_ref[...] = (
        chosen
        + jnp.log(ones * length.astype(F32))
        - jnp.log(ones * (prop_ref[0].astype(F32) / 1024.0))
    )


def body(
    query, item_table, context_features, candidates, lengths, logged_slot, logging_prop,
    w_first, w_second, w_score,
):
    item_rows, width = item_table.shape
    slots = candidates.shape[1]
    feature_width = context_features.shape[1]
    chips = lax.axis_size(CHIPS)
    plane = lax.axis_size(("x", "z"))
    message = width + feature_width + 256
    vmem = pl.BlockSpec(memory_space=pltpu.VMEM)
    smem = pl.BlockSpec(memory_space=pltpu.SMEM)

    tables = lax.all_gather(item_table, "core", axis=0, tiled=False)
    payload, pick = pl.pallas_call(
        lambda *refs: ask_kernel(plane, chips, item_rows, *refs),
        out_shape=(
            jax.ShapeDtypeStruct((chips, message), BF),
            jax.ShapeDtypeStruct((1, slots), jnp.int32),
        ),
        in_specs=[vmem] * 3,
        out_specs=(vmem, vmem),
        name="ask",
    )(query, context_features, candidates)
    asked = lax.all_to_all(
        payload.reshape(chips, message // 128, 128), CHIPS, split_axis=0, concat_axis=0, tiled=True
    ).reshape(chips, message)
    answers = pl.pallas_call(
        hold_kernel,
        out_shape=jax.ShapeDtypeStruct((chips, 128), F32),
        in_specs=[vmem] * 5,
        out_specs=vmem,
        scratch_shapes=[pltpu.VMEM((chips, 2 * item_rows), F32)],
        compiler_params=pltpu.CompilerParams(vmem_limit_bytes=40 * 1024 * 1024),
        name="hold",
    )(asked, tables, w_first, w_second, w_score.reshape(1, -1))
    back = lax.all_to_all(
        answers.reshape(chips, 1, 128), CHIPS, split_axis=0, concat_axis=0, tiled=True
    ).reshape(chips, 128)
    total_items = item_rows * 2 * chips
    section, weight = pl.pallas_call(
        lambda *refs: own_kernel(plane, item_rows, total_items, *refs),
        out_shape=(
            jax.ShapeDtypeStruct((1, slots), F32),
            jax.ShapeDtypeStruct((1, 128), F32),
        ),
        in_specs=[vmem] * 3 + [smem] * 3,
        out_specs=(vmem, vmem),
        name="own",
    )(back, candidates, pick, lengths, logged_slot, logging_prop)
    return section, weight[0, :1]


def solution(mesh):
    split = Mesh(mesh.devices.reshape(8, 2, 4, 8), ALL)
    row, flat = P(ALL, None), P(ALL)
    placed = (row, row, row, row, flat, flat, flat, P(), P(), P())
    return jax.shard_map(
        body, mesh=split, in_specs=placed, out_specs=(row, flat), check_vma=False
    )
```

```python
import math

import jax
import jax.numpy as jnp
from jax import lax
from jax.experimental import pallas as pl
from jax.experimental.pallas import tpu as pltpu
from jax.sharding import Mesh
from jax.sharding import PartitionSpec as P

ALL = ("y", "core", "x", "z")
CHIPS = ("y", "x", "z")
BIG = float(1 << 24)
CAP = 3
ROWS = 8
BF = jnp.bfloat16
F32 = jnp.float32


def dot_nt(a, b):
    return lax.dot_general(a, b, (((1,), (1,)), ((), ())), preferred_element_type=F32)


def dot_nn(a, b):
    return lax.dot_general(a, b, (((1,), (0,)), ((), ())), preferred_element_type=F32)


def silu(v):
    half = 0.5 * v
    return half + half * jnp.tanh(half)


def asked_keys(which, plane, chips, item_rows, ids):
    holder = lax.shift_right_logical(ids, item_rows.bit_length() - 1)
    slot = lax.broadcasted_iota(jnp.int32, ids.shape, 1)
    key = (slot * item_rows + (ids & (item_rows - 1))).astype(F32)
    core = lax.axis_index("core") ^ which
    chip = lax.broadcasted_iota(jnp.int32, (chips, 1), 0)
    device = (chip // plane) * (2 * plane) + core * plane + chip % plane
    mine = holder == device
    low = jnp.min(jnp.where(mine, key, BIG), axis=1, keepdims=True)
    high = jnp.max(jnp.where(mine, key, -1.0), axis=1, keepdims=True)
    total = jnp.sum(jnp.where(mine, key, 0.0), axis=1, keepdims=True)
    return key, low, high, total


def ask_kernel(plane, chips, item_rows, query_ref, feature_ref, ids_ref, message_ref):
    ids = ids_ref[...]
    lane = lax.broadcasted_iota(jnp.int32, (chips, 128), 1)
    wanted = jnp.full((chips, 128), -1.0, F32)
    for which in range(2):
        _, low, high, total = asked_keys(which, plane, chips, item_rows, ids)
        middle = total - low - high
        least = jnp.where(high >= 0.0, low, -1.0)
        middle = jnp.where((high > low) & (middle > 0.0), middle, -1.0)
        most = jnp.where(high > low, high, -1.0)
        for j, keys in enumerate((least, middle, most)):
            at = 2 * (which * CAP + j)
            wanted = jnp.where((lane == at) | (lane == at + 1), keys, wanted)
    wanted = wanted.astype(jnp.int32)
    inside = jnp.where(wanted < 0, 2 * item_rows, wanted & (item_rows - 1))
    asked = jnp.where((lane & 1) == 0, lax.shift_right_logical(inside, 8), inside & 255)
    asked = asked.astype(F32).astype(BF)
    row = lax.broadcasted_iota(jnp.int32, (ROWS * chips, chips), 0)
    chip = lax.broadcasted_iota(jnp.int32, (ROWS * chips, chips), 1)
    spread = jnp.where(row == chip * ROWS + ROWS - 2, 1.0, 0.0).astype(BF)
    spread = dot_nn(spread, asked).reshape(chips, ROWS, 128)
    line = lax.broadcasted_iota(jnp.int32, (ROWS, 128), 0)
    own = jnp.zeros((ROWS, 128), F32)
    at = 0
    for ref in (query_ref, feature_ref):
        for k in range(0, ref.shape[1], 128):
            own = jnp.where(line == at, ref[:, k : k + 128].astype(F32), own)
            at += 1
    message_ref[...] = (spread + own[None]).reshape(ROWS * chips, 128).astype(BF)


def place_kernel(plane, chips, item_rows, ids_ref, pick_ref, chosen_ref):
    ids = ids_ref[...]
    first = jnp.zeros(ids.shape, F32)
    last = jnp.zeros(ids.shape, F32)
    for which in range(2):
        key, low, high, _ = asked_keys(which, plane, chips, item_rows, ids)
        first = first + jnp.sum(jnp.where(low == key, 1.0, 0.0), axis=0, keepdims=True)
        last = last + jnp.sum(jnp.where(high == key, 1.0, 0.0), axis=0, keepdims=True)
    place = jnp.where(first > 0.0, 0, jnp.where(last > 0.0, 2, 1))
    holder = lax.shift_right_logical(ids, item_rows.bit_length() - 1)
    pick_ref[...] = (((holder // plane) & 1) ^ lax.axis_index("core")) * CAP + place
    chip_of = (holder // (2 * plane)) * plane + holder % plane
    chip = lax.broadcasted_iota(jnp.int32, chosen_ref.shape, 0)
    chosen_ref[...] = jnp.where(chip == chip_of, 1.0, 0.0).astype(BF)


def hold_kernel(
    asked_ref, own_ref, other_ref, w_first_ref, w_second_ref, w_score_ref, out_ref, logits_ref
):
    contexts = asked_ref.shape[0]
    tables = (own_ref, other_ref)
    item_rows, width = own_ref.shape
    feature_width = w_first_ref.shape[0] - width
    query = asked_ref[:, :width]
    lane = lax.broadcasted_iota(jnp.int32, (contexts, 128), 1)
    chunk = 512
    peak = jnp.full((contexts, 128), -1e30, F32)
    for core in range(2):
        for start in range(0, item_rows, chunk):
            logits = dot_nt(query, tables[core][start : start + chunk, :])
            at = core * item_rows + start
            logits_ref[:, at : at + chunk] = logits
            for k in range(0, chunk, 128):
                peak = jnp.maximum(peak, logits[:, k : k + 128])
    peak = jnp.max(peak, axis=1, keepdims=True)
    total = jnp.zeros((contexts, 128), F32)
    for start in range(0, 2 * item_rows, 128):
        total = total + jnp.exp(logits_ref[:, start : start + 128] - peak)
    total = jnp.sum(total, axis=1, keepdims=True)
    out = jnp.where(lane == 4 * CAP, peak, jnp.where(lane == 4 * CAP + 1, total, 0.0))

    context_part = dot_nn(
        asked_ref[:, width : width + feature_width], w_first_ref[:feature_width, :]
    )
    query_wide = query.astype(F32)
    id_parts = asked_ref[:, width + feature_width :].astype(F32)
    item = lax.broadcasted_iota(jnp.int32, (contexts, item_rows), 1)
    w_score = jnp.broadcast_to(w_score_ref[...], (128, w_score_ref.shape[1]))
    for core in range(2):
        for j in range(CAP):
            place = core * CAP + j
            inside = id_parts[:, 2 * place : 2 * place + 1] * 256.0
            inside = (inside + id_parts[:, 2 * place + 1 : 2 * place + 2]).astype(jnp.int32)
            chosen = jnp.where(item == inside, 1.0, 0.0).astype(BF)
            rows = dot_nn(chosen, tables[core][...])
            gen = jnp.sum(rows * query_wide, axis=1, keepdims=True)
            hidden = silu(dot_nn(rows.astype(BF), w_first_ref[feature_width:, :]) + context_part)
            second = silu(dot_nn(hidden.astype(BF), w_second_ref[...]))
            score = dot_nt(second.astype(BF), w_score)
            out = jnp.where(lane == place, score, out)
            out = jnp.where(lane == 2 * CAP + place, gen, out)
    out_ref[...] = out


def own_kernel(
    total_items,
    back_ref, chosen_ref, pick_ref, length_ref, logged_ref, prop_ref, section_ref, weight_ref,
):
    slots = pick_ref.shape[1]
    back = jnp.transpose(back_ref[...])[:16]
    peaks, sums = back[4 * CAP : 4 * CAP + 1], back[4 * CAP + 1 : 4 * CAP + 2]
    peak = jnp.max(peaks, axis=1, keepdims=True)
    log_norm = peak + jnp.log(jnp.sum(sums * jnp.exp(peaks - peak), axis=1, keepdims=True))
    chosen = chosen_ref[...]
    top = back.astype(BF)
    rest = back - top.astype(F32)
    middle = rest.astype(BF)
    low = (rest - middle.astype(F32)).astype(BF)
    found = dot_nn(top, chosen) + dot_nn(middle, chosen) + dot_nn(low, chosen)
    pick = pick_ref[...]
    score = jnp.zeros((1, slots), F32)
    gen = jnp.zeros((1, slots), F32)
    for place in range(2 * CAP):
        score = jnp.where(pick == place, found[place : place + 1], score)
        gen = jnp.where(pick == place, found[2 * CAP + place : 2 * CAP + place + 1], gen)
    slot = lax.broadcasted_iota(jnp.int32, (1, slots), 1)
    length = length_ref[0]
    live = slot < length
    masked = jnp.where(live, score, -1e30)
    rank_peak = jnp.max(masked, axis=1, keepdims=True)
    rank_sum = jnp.sum(jnp.where(live, jnp.exp(masked - rank_peak), 0.0), axis=1, keepdims=True)
    rank_norm = rank_peak + jnp.log(rank_sum)
    section = jnp.where(live, score - rank_norm + gen - log_norm + math.log(total_items), 0.0)
    section_ref[...] = section
    chosen = jnp.sum(jnp.where(slot == logged_ref[0], section, 0.0), axis=1, keepdims=True)
    ones = jnp.ones((1, 128), F32)
    weight_ref[...] = (
        chosen
        + jnp.log(ones * length.astype(F32))
        - jnp.log(ones * (prop_ref[0].astype(F32) / 1024.0))
    )


def body(
    query, item_table, context_features, candidates, lengths, logged_slot, logging_prop,
    w_first, w_second, w_score,
):
    item_rows, width = item_table.shape
    slots = candidates.shape[1]
    chips = lax.axis_size(CHIPS)
    plane = lax.axis_size(("x", "z"))
    vmem = pl.BlockSpec(memory_space=pltpu.VMEM)
    smem = pl.BlockSpec(memory_space=pltpu.SMEM)

    other_table = lax.ppermute(item_table, "core", [(0, 1), (1, 0)])
    message = pl.pallas_call(
        lambda *refs: ask_kernel(plane, chips, item_rows, *refs),
        out_shape=jax.ShapeDtypeStruct((ROWS * chips, 128), BF),
        in_specs=[vmem] * 3,
        out_specs=vmem,
        name="ask",
    )(query, context_features, candidates)
    asked = lax.all_to_all(
        message.reshape(chips, ROWS, 128), CHIPS, split_axis=0, concat_axis=0, tiled=True
    ).reshape(chips, ROWS * 128)
    pick, chosen = pl.pallas_call(
        lambda *refs: place_kernel(plane, chips, item_rows, *refs),
        out_shape=(
            jax.ShapeDtypeStruct((1, slots), jnp.int32),
            jax.ShapeDtypeStruct((chips, slots), BF),
        ),
        in_specs=[vmem],
        out_specs=(vmem, vmem),
        cost_estimate=pl.CostEstimate(flops=4000000, bytes_accessed=600000, transcendentals=0),
        name="place",
    )(candidates)
    answers = pl.pallas_call(
        hold_kernel,
        out_shape=jax.ShapeDtypeStruct((chips, 128), F32),
        in_specs=[vmem] * 6,
        out_specs=vmem,
        scratch_shapes=[pltpu.VMEM((chips, 2 * item_rows), F32)],
        compiler_params=pltpu.CompilerParams(vmem_limit_bytes=40 * 1024 * 1024),
        name="hold",
    )(asked, item_table, other_table, w_first, w_second, w_score.reshape(1, -1))
    back = lax.all_to_all(
        answers.reshape(chips, 1, 128), CHIPS, split_axis=0, concat_axis=0, tiled=True
    ).reshape(chips, 128)
    total_items = item_rows * 2 * chips
    section, weight = pl.pallas_call(
        lambda *refs: own_kernel(total_items, *refs),
        out_shape=(
            jax.ShapeDtypeStruct((1, slots), F32),
            jax.ShapeDtypeStruct((1, 128), F32),
        ),
        in_specs=[vmem] * 3 + [smem] * 3,
        out_specs=(vmem, vmem),
        name="own",
    )(back, chosen, pick, lengths, logged_slot, logging_prop)
    return section, weight[0, :1]


def solution(mesh):
    split = Mesh(mesh.devices.reshape(8, 2, 4, 8), ALL)
    row, flat = P(ALL, None), P(ALL)
    placed = (row, row, row, row, flat, flat, flat, P(), P(), P())
    return jax.shard_map(
        body, mesh=split, in_specs=placed, out_specs=(row, flat), check_vma=False
    )
```

```python
import math

import jax
import jax.numpy as jnp
from jax import lax
from jax.experimental import pallas as pl
from jax.experimental.pallas import tpu as pltpu
from jax.sharding import Mesh
from jax.sharding import PartitionSpec as P

ALL = ("y", "core", "x", "z")
CHIPS = ("y", "x", "z")
BIG = float(1 << 24)
CAP = 3
ROWS = 8
MIB = 1 << 20
BF = jnp.bfloat16
F32 = jnp.float32


def dot_nt(a, b):
    return lax.dot_general(a, b, (((1,), (1,)), ((), ())), preferred_element_type=F32)


def dot_nn(a, b):
    return lax.dot_general(a, b, (((1,), (0,)), ((), ())), preferred_element_type=F32)


def silu(v):
    half = 0.5 * v
    return half + half * jnp.tanh(half)


def asked_keys(which, plane, chips, item_rows, ids):
    holder = lax.shift_right_logical(ids, item_rows.bit_length() - 1)
    slot = lax.broadcasted_iota(jnp.int32, ids.shape, 1)
    key = (slot * item_rows + (ids & (item_rows - 1))).astype(F32)
    core = lax.axis_index("core") ^ which
    chip = lax.broadcasted_iota(jnp.int32, (chips, 1), 0)
    device = (chip // plane) * (2 * plane) + core * plane + chip % plane
    mine = holder == device
    low = jnp.min(jnp.where(mine, key, BIG), axis=1, keepdims=True)
    high = jnp.max(jnp.where(mine, key, -1.0), axis=1, keepdims=True)
    total = jnp.sum(jnp.where(mine, key, 0.0), axis=1, keepdims=True)
    return key, low, high, total


def ask_kernel(plane, chips, item_rows, query_ref, feature_ref, ids_ref, message_ref, spread_ref):
    ids = ids_ref[...]
    lane = lax.broadcasted_iota(jnp.int32, (chips, 128), 1)
    wanted = jnp.full((chips, 128), -1.0, F32)
    for which in range(2):
        _, low, high, total = asked_keys(which, plane, chips, item_rows, ids)
        middle = total - low - high
        least = jnp.where(high >= 0.0, low, -1.0)
        middle = jnp.where((high > low) & (middle > 0.0), middle, -1.0)
        most = jnp.where(high > low, high, -1.0)
        for j, keys in enumerate((least, middle, most)):
            at = 2 * (which * CAP + j)
            wanted = jnp.where((lane == at) | (lane == at + 1), keys, wanted)
    wanted = wanted.astype(jnp.int32)
    inside = jnp.where(wanted < 0, 2 * item_rows, wanted & (item_rows - 1))
    asked = jnp.where((lane & 1) == 0, lax.shift_right_logical(inside, 8), inside & 255)
    asked = asked.astype(F32)
    spread_ref[pl.ds(ROWS - 2, chips, stride=ROWS), :] = asked
    line = lax.broadcasted_iota(jnp.int32, (ROWS, 128), 0)
    own = jnp.zeros((ROWS, 128), F32)
    at = 0
    for ref in (query_ref, feature_ref):
        for k in range(0, ref.shape[1], 128):
            own = jnp.where(line == at, ref[:, k : k + 128].astype(F32), own)
            at += 1
    spread = spread_ref[...].reshape(chips, ROWS, 128)
    spread = jnp.where((line == ROWS - 2)[None], spread, own[None])
    message_ref[...] = spread.reshape(ROWS * chips, 128).astype(BF)


def place_kernel(
    plane, chips, item_rows, ids_ref, length_ref, logged_ref, prop_ref, facts_ref, chosen_ref
):
    ids = ids_ref[...]
    first = jnp.zeros(ids.shape, F32)
    last = jnp.zeros(ids.shape, F32)
    for which in range(2):
        key, low, high, _ = asked_keys(which, plane, chips, item_rows, ids)
        first = first + jnp.sum(jnp.where(low == key, 1.0, 0.0), axis=0, keepdims=True)
        last = last + jnp.sum(jnp.where(high == key, 1.0, 0.0), axis=0, keepdims=True)
    place = jnp.where(first > 0.0, 0, jnp.where(last > 0.0, 2, 1))
    holder = lax.shift_right_logical(ids, item_rows.bit_length() - 1)
    place = (((holder // plane) & 1) ^ lax.axis_index("core")) * CAP + place
    slot = lax.broadcasted_iota(jnp.int32, ids.shape, 1)
    ones = jnp.ones(ids.shape, F32)
    length = length_ref[0]
    facts_ref[0:1] = place.astype(F32)
    facts_ref[1:2] = jnp.where(slot < length, 1.0, 0.0)
    facts_ref[2:3] = jnp.where(slot == logged_ref[0], 1.0, 0.0)
    facts_ref[3:4] = jnp.log(ones * length.astype(F32)) - jnp.log(
        ones * (prop_ref[0].astype(F32) / 1024.0)
    )
    chip_of = (holder // (2 * plane)) * plane + holder % plane
    chip = lax.broadcasted_iota(jnp.int32, chosen_ref.shape, 0)
    chosen_ref[...] = jnp.where(chip == chip_of, 1.0, 0.0).astype(BF)


def hold_kernel(
    asked_ref, own_ref, other_ref, w_first_ref, w_second_ref, w_score_ref, out_ref, lines_ref
):
    contexts = asked_ref.shape[0] // ROWS
    tables = (own_ref, other_ref)
    item_rows, width = own_ref.shape
    feature_width = w_first_ref.shape[0] - width
    lines_ref[...] = asked_ref[...].astype(F32)
    lines = [lines_ref[pl.ds(k, contexts, stride=ROWS), :] for k in range(ROWS - 1)]
    query_wide = jnp.concatenate(lines[: width // 128], axis=1)
    query = query_wide.astype(BF)
    features = jnp.concatenate(lines[width // 128 : ROWS - 2], axis=1).astype(BF)
    id_parts = lines[ROWS - 2]
    lane = lax.broadcasted_iota(jnp.int32, (contexts, 128), 1)
    chunk = 1024
    peak = jnp.full((contexts, 128), -1e30, F32)
    total = jnp.zeros((contexts, 128), F32)
    for core in range(2):
        for start in range(0, item_rows, chunk):
            logits = dot_nt(query, tables[core][start : start + chunk, :])
            new = peak
            for k in range(0, chunk, 128):
                new = jnp.maximum(new, logits[:, k : k + 128])
            total = total * jnp.exp(peak - new)
            for k in range(0, chunk, 128):
                total = total + jnp.exp(logits[:, k : k + 128] - new)
            peak = new
    top = jnp.max(peak, axis=1, keepdims=True)
    total = jnp.sum(total * jnp.exp(peak - top), axis=1, keepdims=True)
    out = jnp.where(lane == 4 * CAP, top, jnp.where(lane == 4 * CAP + 1, total, 0.0))

    context_part = dot_nn(features, w_first_ref[:feature_width, :])
    item = lax.broadcasted_iota(jnp.int32, (contexts, item_rows), 1)
    w_score = jnp.broadcast_to(w_score_ref[...], (128, w_score_ref.shape[1]))
    for core in range(2):
        for j in range(CAP):
            place = core * CAP + j
            inside = id_parts[:, 2 * place : 2 * place + 1] * 256.0
            inside = (inside + id_parts[:, 2 * place + 1 : 2 * place + 2]).astype(jnp.int32)
            chosen = jnp.where(item == inside, 1.0, 0.0).astype(BF)
            rows = dot_nn(chosen, tables[core][...])
            gen = jnp.sum(rows * query_wide, axis=1, keepdims=True)
            hidden = silu(dot_nn(rows.astype(BF), w_first_ref[feature_width:, :]) + context_part)
            second = silu(dot_nn(hidden.astype(BF), w_second_ref[...]))
            score = dot_nt(second.astype(BF), w_score)
            out = jnp.where(lane == place, score, out)
            out = jnp.where(lane == 2 * CAP + place, gen, out)
    out_ref[...] = out


def own_kernel(total_items, back_ref, chosen_ref, facts_ref, section_ref, weight_ref):
    back = jnp.transpose(back_ref[...])[:16]
    top = back.astype(BF)
    rest = back - top.astype(F32)
    middle = rest.astype(BF)
    low = (rest - middle.astype(F32)).astype(BF)
    found = dot_nn(jnp.concatenate([top, middle, low], axis=0), chosen_ref[...])
    found = found[:16] + found[16:32] + found[32:]
    peaks, sums = back[4 * CAP : 4 * CAP + 1], back[4 * CAP + 1 : 4 * CAP + 2]
    peak = jnp.max(peaks, axis=1, keepdims=True)
    log_norm = peak + jnp.log(jnp.sum(sums * jnp.exp(peaks - peak), axis=1, keepdims=True))
    place = facts_ref[0:1]
    live = facts_ref[1:2] > 0.0
    score = jnp.zeros(place.shape, F32)
    gen = jnp.zeros(place.shape, F32)
    for k in range(2 * CAP):
        score = jnp.where(place == k, found[k : k + 1], score)
        gen = jnp.where(place == k, found[2 * CAP + k : 2 * CAP + k + 1], gen)
    masked = jnp.where(live, score, -1e30)
    rank_peak = jnp.max(masked, axis=1, keepdims=True)
    rank_sum = jnp.sum(jnp.where(live, jnp.exp(masked - rank_peak), 0.0), axis=1, keepdims=True)
    rank_norm = rank_peak + jnp.log(rank_sum)
    section = jnp.where(live, score - rank_norm + gen - log_norm + math.log(total_items), 0.0)
    section_ref[...] = section
    chosen = jnp.sum(jnp.where(facts_ref[2:3] > 0.0, section, 0.0), axis=1, keepdims=True)
    weight_ref[...] = chosen + facts_ref[3:4, :128]


def body(
    query, item_table, context_features, candidates, lengths, logged_slot, logging_prop,
    w_first, w_second, w_score,
):
    item_rows, width = item_table.shape
    slots = candidates.shape[1]
    chips = lax.axis_size(CHIPS)
    plane = lax.axis_size(("x", "z"))
    vmem = pl.BlockSpec(memory_space=pltpu.VMEM)
    smem = pl.BlockSpec(memory_space=pltpu.SMEM)

    message = pl.pallas_call(
        lambda *refs: ask_kernel(plane, chips, item_rows, *refs),
        out_shape=jax.ShapeDtypeStruct((ROWS * chips, 128), BF),
        in_specs=[vmem] * 3,
        out_specs=vmem,
        scratch_shapes=[pltpu.VMEM((ROWS * chips, 128), F32)],
        compiler_params=pltpu.CompilerParams(vmem_limit_bytes=60 * MIB),
        name="ask",
    )(query, context_features, candidates)
    other_table = lax.ppermute(item_table, "core", [(0, 1), (1, 0)])
    asked = lax.all_to_all(
        message.reshape(chips, ROWS, 128), CHIPS, split_axis=0, concat_axis=0, tiled=True
    ).reshape(ROWS * chips, 128)
    facts, chosen = pl.pallas_call(
        lambda *refs: place_kernel(plane, chips, item_rows, *refs),
        out_shape=(
            jax.ShapeDtypeStruct((8, slots), F32),
            jax.ShapeDtypeStruct((chips, slots), BF),
        ),
        in_specs=[vmem] + [smem] * 3,
        out_specs=(vmem, vmem),
        compiler_params=pltpu.CompilerParams(vmem_limit_bytes=8 * MIB),
        cost_estimate=pl.CostEstimate(flops=20000000000, bytes_accessed=600000, transcendentals=0),
        name="place",
    )(candidates, lengths, logged_slot, logging_prop)
    asked, facts = lax.optimization_barrier((asked, facts))
    answers = pl.pallas_call(
        hold_kernel,
        out_shape=jax.ShapeDtypeStruct((chips, 128), F32),
        in_specs=[vmem] * 6,
        out_specs=vmem,
        scratch_shapes=[pltpu.VMEM((ROWS * chips, 128), F32)],
        compiler_params=pltpu.CompilerParams(vmem_limit_bytes=16 * MIB),
        name="hold",
    )(asked, item_table, other_table, w_first, w_second, w_score.reshape(1, -1))
    back = lax.all_to_all(
        answers.reshape(chips, 1, 128), CHIPS, split_axis=0, concat_axis=0, tiled=True
    ).reshape(chips, 128)
    total_items = item_rows * 2 * chips
    section, weight = pl.pallas_call(
        lambda *refs: own_kernel(total_items, *refs),
        out_shape=(
            jax.ShapeDtypeStruct((1, slots), F32),
            jax.ShapeDtypeStruct((1, 128), F32),
        ),
        in_specs=[vmem] * 3,
        out_specs=(vmem, vmem),
        compiler_params=pltpu.CompilerParams(vmem_limit_bytes=8 * MIB),
        name="own",
    )(back, chosen, facts)
    return section, weight[0, :1]


def solution(mesh):
    split = Mesh(mesh.devices.reshape(8, 2, 4, 8), ALL)
    row, flat = P(ALL, None), P(ALL)
    placed = (row, row, row, row, flat, flat, flat, P(), P(), P())
    return jax.shard_map(
        body, mesh=split, in_specs=placed, out_specs=(row, flat), check_vma=False
    )
```

```python
import math

import jax
import jax.numpy as jnp
from jax import lax
from jax.experimental import pallas as pl
from jax.experimental.pallas import tpu as pltpu
from jax.sharding import Mesh
from jax.sharding import PartitionSpec as P

ALL = ("y", "core", "x", "z")
CHIPS = ("y", "x", "z")
BIG = float(1 << 24)
CAP = 3
ROWS = 8
MIB = 1 << 20
BF = jnp.bfloat16
F32 = jnp.float32


def dot_nt(a, b):
    return lax.dot_general(a, b, (((1,), (1,)), ((), ())), preferred_element_type=F32)


def dot_nn(a, b):
    return lax.dot_general(a, b, (((1,), (0,)), ((), ())), preferred_element_type=F32)


def silu(v):
    half = 0.5 * v
    return half + half * jnp.tanh(half)


def asked_keys(which, plane, chips, item_rows, ids):
    holder = lax.shift_right_logical(ids, item_rows.bit_length() - 1)
    slot = lax.broadcasted_iota(jnp.int32, ids.shape, 1)
    key = (slot * item_rows + (ids & (item_rows - 1))).astype(F32)
    core = lax.axis_index("core") ^ which
    chip = lax.broadcasted_iota(jnp.int32, (chips, 1), 0)
    device = (chip // plane) * (2 * plane) + core * plane + chip % plane
    mine = holder == device
    low = jnp.min(jnp.where(mine, key, BIG), axis=1, keepdims=True)
    high = jnp.max(jnp.where(mine, key, -1.0), axis=1, keepdims=True)
    total = jnp.sum(jnp.where(mine, key, 0.0), axis=1, keepdims=True)
    return key, low, high, total


def ask_kernel(plane, chips, item_rows, query_ref, feature_ref, ids_ref, message_ref, spread_ref):
    ids = ids_ref[...]
    lane = lax.broadcasted_iota(jnp.int32, (chips, 128), 1)
    wanted = jnp.full((chips, 128), -1.0, F32)
    for which in range(2):
        _, low, high, total = asked_keys(which, plane, chips, item_rows, ids)
        middle = total - low - high
        least = jnp.where(high >= 0.0, low, -1.0)
        middle = jnp.where((high > low) & (middle > 0.0), middle, -1.0)
        most = jnp.where(high > low, high, -1.0)
        for j, keys in enumerate((least, middle, most)):
            at = 2 * (which * CAP + j)
            wanted = jnp.where((lane == at) | (lane == at + 1), keys, wanted)
    wanted = wanted.astype(jnp.int32)
    inside = jnp.where(wanted < 0, 2 * item_rows, wanted & (item_rows - 1))
    asked = jnp.where((lane & 1) == 0, lax.shift_right_logical(inside, 8), inside & 255)
    asked = asked.astype(F32)
    spread_ref[pl.ds(ROWS - 2, chips, stride=ROWS), :] = asked
    line = lax.broadcasted_iota(jnp.int32, (ROWS, 128), 0)
    own = jnp.zeros((ROWS, 128), F32)
    at = 0
    for ref in (query_ref, feature_ref):
        for k in range(0, ref.shape[1], 128):
            own = jnp.where(line == at, ref[:, k : k + 128].astype(F32), own)
            at += 1
    spread = spread_ref[...].reshape(chips, ROWS, 128)
    spread = jnp.where((line == ROWS - 2)[None], spread, own[None])
    message_ref[...] = spread.reshape(ROWS * chips, 128).astype(BF)


def place_kernel(
    plane, chips, item_rows, ids_ref, length_ref, logged_ref, prop_ref, facts_ref, chosen_ref
):
    ids = ids_ref[...]
    first = jnp.zeros(ids.shape, F32)
    last = jnp.zeros(ids.shape, F32)
    for which in range(2):
        key, low, high, _ = asked_keys(which, plane, chips, item_rows, ids)
        first = first + jnp.sum(jnp.where(low == key, 1.0, 0.0), axis=0, keepdims=True)
        last = last + jnp.sum(jnp.where(high == key, 1.0, 0.0), axis=0, keepdims=True)
    place = jnp.where(first > 0.0, 0, jnp.where(last > 0.0, 2, 1))
    holder = lax.shift_right_logical(ids, item_rows.bit_length() - 1)
    place = (((holder // plane) & 1) ^ lax.axis_index("core")) * CAP + place
    slot = lax.broadcasted_iota(jnp.int32, ids.shape, 1)
    ones = jnp.ones(ids.shape, F32)
    length = length_ref[0]
    facts_ref[0:1] = place.astype(F32)
    facts_ref[1:2] = jnp.where(slot < length, 1.0, 0.0)
    facts_ref[2:3] = jnp.where(slot == logged_ref[0], 1.0, 0.0)
    facts_ref[3:4] = jnp.log(ones * length.astype(F32)) - jnp.log(
        ones * (prop_ref[0].astype(F32) / 1024.0)
    )
    chip_of = (holder // (2 * plane)) * plane + holder % plane
    chip = lax.broadcasted_iota(jnp.int32, chosen_ref.shape, 0)
    chosen_ref[...] = jnp.where(chip == chip_of, 1.0, 0.0).astype(BF)


def hold_kernel(
    asked_ref, own_ref, other_hbm, w_first_ref, w_second_ref, w_score_ref,
    out_ref, lines_ref, other_ref, other_sem,
):
    other_copy = pltpu.make_async_copy(other_hbm, other_ref, other_sem)
    other_copy.start()
    contexts = asked_ref.shape[0] // ROWS
    tables = (own_ref, other_ref)
    item_rows, width = own_ref.shape
    feature_width = w_first_ref.shape[0] - width
    lines_ref[...] = asked_ref[...].astype(F32)
    lines = [lines_ref[pl.ds(k, contexts, stride=ROWS), :] for k in range(ROWS - 1)]
    query_wide = jnp.concatenate(lines[: width // 128], axis=1)
    query = query_wide.astype(BF)
    features = jnp.concatenate(lines[width // 128 : ROWS - 2], axis=1).astype(BF)
    id_parts = lines[ROWS - 2]
    lane = lax.broadcasted_iota(jnp.int32, (contexts, 128), 1)
    chunk = 1024
    peak = jnp.full((contexts, 128), -1e30, F32)
    total = jnp.zeros((contexts, 128), F32)
    out = jnp.zeros((contexts, 128), F32)
    context_part = dot_nn(features, w_first_ref[:feature_width, :])
    item = lax.broadcasted_iota(jnp.int32, (contexts, item_rows), 1)
    w_score = jnp.broadcast_to(w_score_ref[...], (128, w_score_ref.shape[1]))
    for core in range(2):
        if core == 1:
            other_copy.wait()
        for start in range(0, item_rows, chunk):
            logits = dot_nt(query, tables[core][start : start + chunk, :])
            new = peak
            for k in range(0, chunk, 128):
                new = jnp.maximum(new, logits[:, k : k + 128])
            total = total * jnp.exp(peak - new)
            for k in range(0, chunk, 128):
                total = total + jnp.exp(logits[:, k : k + 128] - new)
            peak = new
        for j in range(CAP):
            place = core * CAP + j
            inside = id_parts[:, 2 * place : 2 * place + 1] * 256.0
            inside = (inside + id_parts[:, 2 * place + 1 : 2 * place + 2]).astype(jnp.int32)
            chosen = jnp.where(item == inside, 1.0, 0.0).astype(BF)
            rows = dot_nn(chosen, tables[core][...])
            gen = jnp.sum(rows * query_wide, axis=1, keepdims=True)
            hidden = silu(dot_nn(rows.astype(BF), w_first_ref[feature_width:, :]) + context_part)
            second = silu(dot_nn(hidden.astype(BF), w_second_ref[...]))
            score = dot_nt(second.astype(BF), w_score)
            out = jnp.where(lane == place, score, out)
            out = jnp.where(lane == 2 * CAP + place, gen, out)
    top = jnp.max(peak, axis=1, keepdims=True)
    total = jnp.sum(total * jnp.exp(peak - top), axis=1, keepdims=True)
    out = jnp.where(lane == 4 * CAP, top, jnp.where(lane == 4 * CAP + 1, total, out))
    out_ref[...] = out


def own_kernel(total_items, back_ref, chosen_ref, facts_ref, section_ref, weight_ref):
    back = jnp.transpose(back_ref[...])[:16]
    top = back.astype(BF)
    rest = back - top.astype(F32)
    middle = rest.astype(BF)
    low = (rest - middle.astype(F32)).astype(BF)
    found = dot_nn(jnp.concatenate([top, middle, low], axis=0), chosen_ref[...])
    found = found[:16] + found[16:32] + found[32:]
    peaks, sums = back[4 * CAP : 4 * CAP + 1], back[4 * CAP + 1 : 4 * CAP + 2]
    peak = jnp.max(peaks, axis=1, keepdims=True)
    log_norm = peak + jnp.log(jnp.sum(sums * jnp.exp(peaks - peak), axis=1, keepdims=True))
    place = facts_ref[0:1]
    live = facts_ref[1:2] > 0.0
    score = jnp.zeros(place.shape, F32)
    gen = jnp.zeros(place.shape, F32)
    for k in range(2 * CAP):
        score = jnp.where(place == k, found[k : k + 1], score)
        gen = jnp.where(place == k, found[2 * CAP + k : 2 * CAP + k + 1], gen)
    masked = jnp.where(live, score, -1e30)
    rank_peak = jnp.max(masked, axis=1, keepdims=True)
    rank_sum = jnp.sum(jnp.where(live, jnp.exp(masked - rank_peak), 0.0), axis=1, keepdims=True)
    rank_norm = rank_peak + jnp.log(rank_sum)
    section = jnp.where(live, score - rank_norm + gen - log_norm + math.log(total_items), 0.0)
    section_ref[...] = section
    chosen = jnp.sum(jnp.where(facts_ref[2:3] > 0.0, section, 0.0), axis=1, keepdims=True)
    weight_ref[...] = chosen + facts_ref[3:4, :128]


def body(
    query, item_table, context_features, candidates, lengths, logged_slot, logging_prop,
    w_first, w_second, w_score,
):
    item_rows, width = item_table.shape
    slots = candidates.shape[1]
    chips = lax.axis_size(CHIPS)
    plane = lax.axis_size(("x", "z"))
    vmem = pl.BlockSpec(memory_space=pltpu.VMEM)
    smem = pl.BlockSpec(memory_space=pltpu.SMEM)

    message = pl.pallas_call(
        lambda *refs: ask_kernel(plane, chips, item_rows, *refs),
        out_shape=jax.ShapeDtypeStruct((ROWS * chips, 128), BF),
        in_specs=[vmem] * 3,
        out_specs=vmem,
        scratch_shapes=[pltpu.VMEM((ROWS * chips, 128), F32)],
        compiler_params=pltpu.CompilerParams(vmem_limit_bytes=60 * MIB),
        name="ask",
    )(query, context_features, candidates)
    other_table = lax.ppermute(item_table, "core", [(0, 1), (1, 0)])
    asked = lax.all_to_all(
        message.reshape(chips, ROWS, 128), CHIPS, split_axis=0, concat_axis=0, tiled=True
    ).reshape(ROWS * chips, 128)
    facts, chosen = pl.pallas_call(
        lambda *refs: place_kernel(plane, chips, item_rows, *refs),
        out_shape=(
            jax.ShapeDtypeStruct((8, slots), F32),
            jax.ShapeDtypeStruct((chips, slots), BF),
        ),
        in_specs=[vmem] + [smem] * 3,
        out_specs=(vmem, vmem),
        compiler_params=pltpu.CompilerParams(vmem_limit_bytes=8 * MIB),
        cost_estimate=pl.CostEstimate(flops=20000000000, bytes_accessed=600000, transcendentals=0),
        name="place",
    )(candidates, lengths, logged_slot, logging_prop)
    asked, facts = lax.optimization_barrier((asked, facts))
    answers = pl.pallas_call(
        hold_kernel,
        out_shape=jax.ShapeDtypeStruct((chips, 128), F32),
        in_specs=[vmem, vmem, pl.BlockSpec(memory_space=pl.ANY), vmem, vmem, vmem],
        out_specs=vmem,
        scratch_shapes=[
            pltpu.VMEM((ROWS * chips, 128), F32),
            pltpu.VMEM(item_table.shape, BF),
            pltpu.SemaphoreType.DMA,
        ],
        compiler_params=pltpu.CompilerParams(vmem_limit_bytes=51 * MIB),
        name="hold",
    )(asked, item_table, other_table, w_first, w_second, w_score.reshape(1, -1))
    back = lax.all_to_all(
        answers.reshape(chips, 1, 128), CHIPS, split_axis=0, concat_axis=0, tiled=True
    ).reshape(chips, 128)
    total_items = item_rows * 2 * chips
    section, weight = pl.pallas_call(
        lambda *refs: own_kernel(total_items, *refs),
        out_shape=(
            jax.ShapeDtypeStruct((1, slots), F32),
            jax.ShapeDtypeStruct((1, 128), F32),
        ),
        in_specs=[vmem] * 3,
        out_specs=(vmem, vmem),
        compiler_params=pltpu.CompilerParams(vmem_limit_bytes=8 * MIB),
        name="own",
    )(back, chosen, facts)
    return section, weight[0, :1]


def solution(mesh):
    split = Mesh(mesh.devices.reshape(8, 2, 4, 8), ALL)
    row, flat = P(ALL, None), P(ALL)
    placed = (row, row, row, row, flat, flat, flat, P(), P(), P())
    return jax.shard_map(
        body, mesh=split, in_specs=placed, out_specs=(row, flat), check_vma=False
    )
```

```python
import math

import jax
import jax.numpy as jnp
from jax import lax
from jax.experimental import pallas as pl
from jax.experimental.pallas import tpu as pltpu
from jax.sharding import Mesh
from jax.sharding import PartitionSpec as P

ALL = ("y", "core", "pair", "side", "z")
GROUPS = ("y", "pair", "z")
FOUR = 4
KEPT = 32
BIG = float(1 << 24)
CAP = 3
ROWS = 8
MIB = 1 << 20
BF = jnp.bfloat16
F32 = jnp.float32


def dot_nt(a, b):
    return lax.dot_general(a, b, (((1,), (1,)), ((), ())), preferred_element_type=F32)


def dot_nn(a, b):
    return lax.dot_general(a, b, (((1,), (0,)), ((), ())), preferred_element_type=F32)


def silu(v):
    half = 0.5 * v
    return half + half * jnp.tanh(half)


def asked_keys(which, shape, groups, item_rows, ids):
    pairs, depth = shape
    holder = lax.shift_right_logical(ids, item_rows.bit_length() - 1)
    slot = lax.broadcasted_iota(jnp.int32, ids.shape, 1)
    key = (slot * item_rows + (ids & (item_rows - 1))).astype(F32)
    core = lax.axis_index("core") ^ (which & 1)
    side = lax.axis_index("side") ^ (which >> 1)
    group = lax.broadcasted_iota(jnp.int32, (groups, 1), 0)
    device = ((group // (pairs * depth)) * 2 + core) * pairs + (group // depth) % pairs
    device = (device * 2 + side) * depth + group % depth
    mine = holder == device
    low = jnp.min(jnp.where(mine, key, BIG), axis=1, keepdims=True)
    high = jnp.max(jnp.where(mine, key, -1.0), axis=1, keepdims=True)
    total = jnp.sum(jnp.where(mine, key, 0.0), axis=1, keepdims=True)
    return key, low, high, total


def ask_kernel(shape, groups, item_rows, query_ref, feature_ref, ids_ref, message_ref, spread_ref):
    ids = ids_ref[...]
    lane = lax.broadcasted_iota(jnp.int32, (groups, 128), 1)
    wanted = jnp.full((groups, 128), -1.0, F32)
    for which in range(FOUR):
        _, low, high, total = asked_keys(which, shape, groups, item_rows, ids)
        middle = total - low - high
        least = jnp.where(high >= 0.0, low, -1.0)
        middle = jnp.where((high > low) & (middle > 0.0), middle, -1.0)
        most = jnp.where(high > low, high, -1.0)
        for j, keys in enumerate((least, middle, most)):
            at = 2 * (which * CAP + j)
            wanted = jnp.where((lane == at) | (lane == at + 1), keys, wanted)
    wanted = wanted.astype(jnp.int32)
    inside = jnp.where(wanted < 0, 2 * item_rows, wanted & (item_rows - 1))
    asked = jnp.where((lane & 1) == 0, lax.shift_right_logical(inside, 8), inside & 255)
    asked = asked.astype(F32)
    spread_ref[pl.ds(ROWS - 2, groups, stride=ROWS), :] = asked
    line = lax.broadcasted_iota(jnp.int32, (ROWS, 128), 0)
    own = jnp.zeros((ROWS, 128), F32)
    at = 0
    for ref in (query_ref, feature_ref):
        for k in range(0, ref.shape[1], 128):
            own = jnp.where(line == at, ref[:, k : k + 128].astype(F32), own)
            at += 1
    spread = spread_ref[...].reshape(groups, ROWS, 128)
    spread = jnp.where((line == ROWS - 2)[None], spread, own[None])
    message_ref[...] = spread.reshape(ROWS * groups, 128).astype(BF)


def place_kernel(
    shape, groups, item_rows, ids_ref, length_ref, logged_ref, prop_ref, facts_ref, chosen_ref
):
    ids = ids_ref[...]
    first = jnp.zeros(ids.shape, F32)
    last = jnp.zeros(ids.shape, F32)
    for which in range(FOUR):
        key, low, high, _ = asked_keys(which, shape, groups, item_rows, ids)
        first = first + jnp.sum(jnp.where(low == key, 1.0, 0.0), axis=0, keepdims=True)
        last = last + jnp.sum(jnp.where(high == key, 1.0, 0.0), axis=0, keepdims=True)
    place = jnp.where(first > 0.0, 0, jnp.where(last > 0.0, 2, 1))
    holder = lax.shift_right_logical(ids, item_rows.bit_length() - 1)
    pairs, depth = shape
    which = ((holder // (2 * depth * pairs)) & 1) ^ lax.axis_index("core")
    which = which + 2 * (((holder // depth) & 1) ^ lax.axis_index("side"))
    place = which * CAP + place
    slot = lax.broadcasted_iota(jnp.int32, ids.shape, 1)
    ones = jnp.ones(ids.shape, F32)
    length = length_ref[0]
    facts_ref[0:1] = place.astype(F32)
    facts_ref[1:2] = jnp.where(slot < length, 1.0, 0.0)
    facts_ref[2:3] = jnp.where(slot == logged_ref[0], 1.0, 0.0)
    facts_ref[3:4] = jnp.log(ones * length.astype(F32)) - jnp.log(
        ones * (prop_ref[0].astype(F32) / 1024.0)
    )
    group_of = (holder // (4 * depth * pairs)) * pairs + (holder // (2 * depth)) % pairs
    group_of = group_of * depth + holder % depth
    group = lax.broadcasted_iota(jnp.int32, chosen_ref.shape, 0)
    chosen_ref[...] = jnp.where(group == group_of, 1.0, 0.0).astype(BF)


def hold_kernel(
    asked_ref, own_ref, second_hbm, third_hbm, fourth_hbm, w_first_ref, w_second_ref, w_score_ref,
    out_ref, lines_ref, second_ref, third_ref, fourth_ref, sems,
):
    copies = (
        None,
        pltpu.make_async_copy(second_hbm, second_ref, sems.at[0]),
        pltpu.make_async_copy(third_hbm, third_ref, sems.at[1]),
        pltpu.make_async_copy(fourth_hbm, fourth_ref, sems.at[2]),
    )
    for copy in copies[1:]:
        copy.start()
    contexts = asked_ref.shape[0] // ROWS
    tables = (own_ref, second_ref, third_ref, fourth_ref)
    item_rows, width = own_ref.shape
    feature_width = w_first_ref.shape[0] - width
    lines_ref[...] = asked_ref[...].astype(F32)
    lines = [lines_ref[pl.ds(k, contexts, stride=ROWS), :] for k in range(ROWS - 1)]
    query_wide = jnp.concatenate(lines[: width // 128], axis=1)
    query = query_wide.astype(BF)
    features = jnp.concatenate(lines[width // 128 : ROWS - 2], axis=1).astype(BF)
    id_parts = lines[ROWS - 2]
    lane = lax.broadcasted_iota(jnp.int32, (contexts, 128), 1)
    chunk = 1024
    peak = jnp.full((contexts, 128), -1e30, F32)
    total = jnp.zeros((contexts, 128), F32)
    out = jnp.zeros((contexts, 128), F32)
    context_part = dot_nn(features, w_first_ref[:feature_width, :])
    context_part = jnp.concatenate([context_part] * CAP, axis=0)
    item = lax.broadcasted_iota(jnp.int32, (CAP * contexts, item_rows), 1)
    w_score = jnp.broadcast_to(w_score_ref[...], (128, w_score_ref.shape[1]))
    for which in range(FOUR):
        if copies[which] is not None:
            copies[which].wait()
        table = tables[which]
        for start in range(0, item_rows, chunk):
            logits = dot_nt(query, table[start : start + chunk, :])
            new = peak
            for k in range(0, chunk, 128):
                new = jnp.maximum(new, logits[:, k : k + 128])
            total = total * jnp.exp(peak - new)
            for k in range(0, chunk, 128):
                total = total + jnp.exp(logits[:, k : k + 128] - new)
            peak = new
        at = 2 * which * CAP
        inside = jnp.concatenate(
            [
                id_parts[:, at + 2 * j : at + 2 * j + 1] * 256.0
                + id_parts[:, at + 2 * j + 1 : at + 2 * j + 2]
                for j in range(CAP)
            ],
            axis=0,
        ).astype(jnp.int32)
        chosen = jnp.where(item == inside, 1.0, 0.0).astype(BF)
        rows = dot_nn(chosen, table[...])
        hidden = silu(dot_nn(rows.astype(BF), w_first_ref[feature_width:, :]) + context_part)
        second = silu(dot_nn(hidden.astype(BF), w_second_ref[...]))
        score = dot_nt(second.astype(BF), w_score)
        for j in range(CAP):
            mine = slice(j * contexts, (j + 1) * contexts)
            gen = jnp.sum(rows[mine] * query_wide, axis=1, keepdims=True)
            place = which * CAP + j
            out = jnp.where(lane == place, score[mine], out)
            out = jnp.where(lane == FOUR * CAP + place, gen, out)
    top = jnp.max(peak, axis=1, keepdims=True)
    total = jnp.sum(total * jnp.exp(peak - top), axis=1, keepdims=True)
    out = jnp.where(lane == 2 * FOUR * CAP, top, jnp.where(lane == 2 * FOUR * CAP + 1, total, out))
    out_ref[...] = out


def own_kernel(total_items, back_ref, chosen_ref, facts_ref, section_ref, weight_ref):
    back = jnp.transpose(back_ref[...])[:KEPT]
    top = back.astype(BF)
    rest = back - top.astype(F32)
    middle = rest.astype(BF)
    low = (rest - middle.astype(F32)).astype(BF)
    found = dot_nn(jnp.concatenate([top, middle, low], axis=0), chosen_ref[...])
    found = found[:KEPT] + found[KEPT : 2 * KEPT] + found[2 * KEPT :]
    at = 2 * FOUR * CAP
    peaks, sums = back[at : at + 1], back[at + 1 : at + 2]
    peak = jnp.max(peaks, axis=1, keepdims=True)
    log_norm = peak + jnp.log(jnp.sum(sums * jnp.exp(peaks - peak), axis=1, keepdims=True))
    place = facts_ref[0:1]
    live = facts_ref[1:2] > 0.0
    score = jnp.zeros(place.shape, F32)
    gen = jnp.zeros(place.shape, F32)
    for k in range(FOUR * CAP):
        score = jnp.where(place == k, found[k : k + 1], score)
        gen = jnp.where(place == k, found[FOUR * CAP + k : FOUR * CAP + k + 1], gen)
    masked = jnp.where(live, score, -1e30)
    rank_peak = jnp.max(masked, axis=1, keepdims=True)
    rank_sum = jnp.sum(jnp.where(live, jnp.exp(masked - rank_peak), 0.0), axis=1, keepdims=True)
    rank_norm = rank_peak + jnp.log(rank_sum)
    section = jnp.where(live, score - rank_norm + gen - log_norm + math.log(total_items), 0.0)
    section_ref[...] = section
    chosen = jnp.sum(jnp.where(facts_ref[2:3] > 0.0, section, 0.0), axis=1, keepdims=True)
    weight_ref[...] = chosen + facts_ref[3:4, :128]


def body(
    query, item_table, context_features, candidates, lengths, logged_slot, logging_prop,
    w_first, w_second, w_score,
):
    item_rows, width = item_table.shape
    slots = candidates.shape[1]
    groups = lax.axis_size(GROUPS)
    shape = (lax.axis_size("pair"), lax.axis_size("z"))
    vmem = pl.BlockSpec(memory_space=pltpu.VMEM)
    smem = pl.BlockSpec(memory_space=pltpu.SMEM)

    third = lax.ppermute(item_table, "side", [(0, 1), (1, 0)])
    message = pl.pallas_call(
        lambda *refs: ask_kernel(shape, groups, item_rows, *refs),
        out_shape=jax.ShapeDtypeStruct((ROWS * groups, 128), BF),
        in_specs=[vmem] * 3,
        out_specs=vmem,
        scratch_shapes=[pltpu.VMEM((ROWS * groups, 128), F32)],
        compiler_params=pltpu.CompilerParams(vmem_limit_bytes=60 * MIB),
        name="ask",
    )(query, context_features, candidates)
    tied_table, message = lax.optimization_barrier((item_table, message))
    second = lax.ppermute(tied_table, "core", [(0, 1), (1, 0)])
    asked = lax.all_to_all(
        message.reshape(groups, ROWS, 128), GROUPS, split_axis=0, concat_axis=0, tiled=True
    ).reshape(ROWS * groups, 128)
    facts, chosen = pl.pallas_call(
        lambda *refs: place_kernel(shape, groups, item_rows, *refs),
        out_shape=(
            jax.ShapeDtypeStruct((8, slots), F32),
            jax.ShapeDtypeStruct((groups, slots), BF),
        ),
        in_specs=[vmem] + [smem] * 3,
        out_specs=(vmem, vmem),
        compiler_params=pltpu.CompilerParams(vmem_limit_bytes=8 * MIB),
        cost_estimate=pl.CostEstimate(flops=20000000000, bytes_accessed=600000, transcendentals=0),
        name="place",
    )(candidates, lengths, logged_slot, logging_prop)
    asked, facts = lax.optimization_barrier((asked, facts))
    fourth = lax.ppermute(third, "core", [(0, 1), (1, 0)])
    answers = pl.pallas_call(
        hold_kernel,
        out_shape=jax.ShapeDtypeStruct((groups, 128), F32),
        in_specs=[vmem] * 2 + [pl.BlockSpec(memory_space=pl.ANY)] * 3 + [vmem] * 3,
        out_specs=vmem,
        scratch_shapes=[
            pltpu.VMEM((ROWS * groups, 128), F32),
            pltpu.VMEM(item_table.shape, BF),
            pltpu.VMEM(item_table.shape, BF),
            pltpu.VMEM(item_table.shape, BF),
            pltpu.SemaphoreType.DMA((3,)),
        ],
        compiler_params=pltpu.CompilerParams(vmem_limit_bytes=51 * MIB),
        name="hold",
    )(asked, item_table, second, third, fourth, w_first, w_second, w_score.reshape(1, -1))
    back = lax.all_to_all(
        answers.reshape(groups, 1, 128), GROUPS, split_axis=0, concat_axis=0, tiled=True
    ).reshape(groups, 128)
    total_items = item_rows * FOUR * groups
    section, weight = pl.pallas_call(
        lambda *refs: own_kernel(total_items, *refs),
        out_shape=(
            jax.ShapeDtypeStruct((1, slots), F32),
            jax.ShapeDtypeStruct((1, 128), F32),
        ),
        in_specs=[vmem] * 3,
        out_specs=(vmem, vmem),
        compiler_params=pltpu.CompilerParams(vmem_limit_bytes=8 * MIB),
        name="own",
    )(back, chosen, facts)
    return section, weight[0, :1]


def solution(mesh):
    split = Mesh(mesh.devices.reshape(8, 2, 2, 2, 8), ALL)
    row, flat = P(ALL, None), P(ALL)
    placed = (row, row, row, row, flat, flat, flat, P(), P(), P())
    return jax.shard_map(
        body, mesh=split, in_specs=placed, out_specs=(row, flat), check_vma=False
    )
```

```python
import math

import jax
import jax.numpy as jnp
from jax import lax
from jax.experimental import pallas as pl
from jax.experimental.pallas import tpu as pltpu
from jax.sharding import Mesh
from jax.sharding import PartitionSpec as P

ALL = ("y", "core", "x", "z")
CHIPS = ("z", "y", "x")
BIG = float(1 << 24)
CAP = 3
ROWS = 8
MIB = 1 << 20
BF = jnp.bfloat16
F32 = jnp.float32


def dot_nt(a, b):
    return lax.dot_general(a, b, (((1,), (1,)), ((), ())), preferred_element_type=F32)


def dot_nn(a, b):
    return lax.dot_general(a, b, (((1,), (0,)), ((), ())), preferred_element_type=F32)


def silu(v):
    half = 0.5 * v
    return half + half * jnp.tanh(half)


def asked_keys(which, plane, chips, item_rows, ids):
    holder = lax.shift_right_logical(ids, item_rows.bit_length() - 1)
    slot = lax.broadcasted_iota(jnp.int32, ids.shape, 1)
    key = (slot * item_rows + (ids & (item_rows - 1))).astype(F32)
    core = lax.axis_index("core") ^ which
    chip = lax.broadcasted_iota(jnp.int32, (chips, 1), 0)
    rows, columns, depth = plane
    x, y, z = chip % columns, (chip // columns) % rows, chip // (columns * rows)
    device = ((y * 2 + core) * columns + x) * depth + z
    mine = holder == device
    low = jnp.min(jnp.where(mine, key, BIG), axis=1, keepdims=True)
    high = jnp.max(jnp.where(mine, key, -1.0), axis=1, keepdims=True)
    total = jnp.sum(jnp.where(mine, key, 0.0), axis=1, keepdims=True)
    return key, low, high, total


def ask_kernel(plane, chips, item_rows, query_ref, feature_ref, ids_ref, message_ref, spread_ref):
    ids = ids_ref[...]
    lane = lax.broadcasted_iota(jnp.int32, (chips, 128), 1)
    wanted = jnp.full((chips, 128), -1.0, F32)
    for which in range(2):
        _, low, high, total = asked_keys(which, plane, chips, item_rows, ids)
        middle = total - low - high
        least = jnp.where(high >= 0.0, low, -1.0)
        middle = jnp.where((high > low) & (middle > 0.0), middle, -1.0)
        most = jnp.where(high > low, high, -1.0)
        for j, keys in enumerate((least, middle, most)):
            at = 2 * (which * CAP + j)
            wanted = jnp.where((lane == at) | (lane == at + 1), keys, wanted)
    wanted = wanted.astype(jnp.int32)
    inside = jnp.where(wanted < 0, 2 * item_rows, wanted & (item_rows - 1))
    asked = jnp.where((lane & 1) == 0, lax.shift_right_logical(inside, 8), inside & 255)
    asked = asked.astype(F32)
    spread_ref[pl.ds(ROWS - 2, chips, stride=ROWS), :] = asked
    line = lax.broadcasted_iota(jnp.int32, (ROWS, 128), 0)
    own = jnp.zeros((ROWS, 128), F32)
    at = 0
    for ref in (query_ref, feature_ref):
        for k in range(0, ref.shape[1], 128):
            own = jnp.where(line == at, ref[:, k : k + 128].astype(F32), own)
            at += 1
    spread = spread_ref[...].reshape(chips, ROWS, 128)
    spread = jnp.where((line == ROWS - 2)[None], spread, own[None])
    message_ref[...] = spread.reshape(ROWS * chips, 128).astype(BF)


def place_kernel(
    plane, chips, item_rows, ids_ref, length_ref, logged_ref, prop_ref, facts_ref, chosen_ref
):
    ids = ids_ref[...]
    first = jnp.zeros(ids.shape, F32)
    last = jnp.zeros(ids.shape, F32)
    for which in range(2):
        key, low, high, _ = asked_keys(which, plane, chips, item_rows, ids)
        first = first + jnp.sum(jnp.where(low == key, 1.0, 0.0), axis=0, keepdims=True)
        last = last + jnp.sum(jnp.where(high == key, 1.0, 0.0), axis=0, keepdims=True)
    place = jnp.where(first > 0.0, 0, jnp.where(last > 0.0, 2, 1))
    holder = lax.shift_right_logical(ids, item_rows.bit_length() - 1)
    rows, columns, depth = plane
    place = (((holder // (columns * depth)) & 1) ^ lax.axis_index("core")) * CAP + place
    slot = lax.broadcasted_iota(jnp.int32, ids.shape, 1)
    ones = jnp.ones(ids.shape, F32)
    length = length_ref[0]
    facts_ref[0:1] = place.astype(F32)
    facts_ref[1:2] = jnp.where(slot < length, 1.0, 0.0)
    facts_ref[2:3] = jnp.where(slot == logged_ref[0], 1.0, 0.0)
    facts_ref[3:4] = jnp.log(ones * length.astype(F32)) - jnp.log(
        ones * (prop_ref[0].astype(F32) / 1024.0)
    )
    chip_of = (holder % depth) * rows + holder // (2 * columns * depth)
    chip_of = chip_of * columns + (holder // depth) % columns
    chip = lax.broadcasted_iota(jnp.int32, chosen_ref.shape, 0)
    chosen_ref[...] = jnp.where(chip == chip_of, 1.0, 0.0).astype(BF)


def hold_kernel(
    asked_ref, own_ref, other_hbm, w_first_ref, w_second_ref, w_score_ref,
    out_ref, lines_ref, other_ref, other_sem,
):
    other_copy = pltpu.make_async_copy(other_hbm, other_ref, other_sem)
    other_copy.start()
    contexts = asked_ref.shape[0] // ROWS
    tables = (own_ref, other_ref)
    item_rows, width = own_ref.shape
    feature_width = w_first_ref.shape[0] - width
    lines_ref[...] = asked_ref[...].astype(F32)
    lines = [lines_ref[pl.ds(k, contexts, stride=ROWS), :] for k in range(ROWS - 1)]
    query_wide = jnp.concatenate(lines[: width // 128], axis=1)
    query = query_wide.astype(BF)
    features = jnp.concatenate(lines[width // 128 : ROWS - 2], axis=1).astype(BF)
    id_parts = lines[ROWS - 2]
    lane = lax.broadcasted_iota(jnp.int32, (contexts, 128), 1)
    chunk = 1024
    peak = jnp.full((contexts, 128), -1e30, F32)
    total = jnp.zeros((contexts, 128), F32)
    out = jnp.zeros((contexts, 128), F32)
    context_part = dot_nn(features, w_first_ref[:feature_width, :])
    item = lax.broadcasted_iota(jnp.int32, (contexts, item_rows), 1)
    w_score = jnp.broadcast_to(w_score_ref[...], (128, w_score_ref.shape[1]))
    for core in range(2):
        if core == 1:
            other_copy.wait()
        for start in range(0, item_rows, chunk):
            logits = dot_nt(query, tables[core][start : start + chunk, :])
            new = peak
            for k in range(0, chunk, 128):
                new = jnp.maximum(new, logits[:, k : k + 128])
            total = total * jnp.exp(peak - new)
            for k in range(0, chunk, 128):
                total = total + jnp.exp(logits[:, k : k + 128] - new)
            peak = new
        for j in range(CAP):
            place = core * CAP + j
            inside = id_parts[:, 2 * place : 2 * place + 1] * 256.0
            inside = (inside + id_parts[:, 2 * place + 1 : 2 * place + 2]).astype(jnp.int32)
            chosen = jnp.where(item == inside, 1.0, 0.0).astype(BF)
            rows = dot_nn(chosen, tables[core][...])
            gen = jnp.sum(rows * query_wide, axis=1, keepdims=True)
            hidden = silu(dot_nn(rows.astype(BF), w_first_ref[feature_width:, :]) + context_part)
            second = silu(dot_nn(hidden.astype(BF), w_second_ref[...]))
            score = dot_nt(second.astype(BF), w_score)
            out = jnp.where(lane == place, score, out)
            out = jnp.where(lane == 2 * CAP + place, gen, out)
    top = jnp.max(peak, axis=1, keepdims=True)
    total = jnp.sum(total * jnp.exp(peak - top), axis=1, keepdims=True)
    out = jnp.where(lane == 4 * CAP, top, jnp.where(lane == 4 * CAP + 1, total, out))
    out_ref[...] = out


def own_kernel(total_items, back_ref, chosen_ref, facts_ref, section_ref, weight_ref):
    back = jnp.transpose(back_ref[...])[:16]
    top = back.astype(BF)
    rest = back - top.astype(F32)
    middle = rest.astype(BF)
    low = (rest - middle.astype(F32)).astype(BF)
    found = dot_nn(jnp.concatenate([top, middle, low], axis=0), chosen_ref[...])
    found = found[:16] + found[16:32] + found[32:]
    peaks, sums = back[4 * CAP : 4 * CAP + 1], back[4 * CAP + 1 : 4 * CAP + 2]
    peak = jnp.max(peaks, axis=1, keepdims=True)
    log_norm = peak + jnp.log(jnp.sum(sums * jnp.exp(peaks - peak), axis=1, keepdims=True))
    place = facts_ref[0:1]
    live = facts_ref[1:2] > 0.0
    score = jnp.zeros(place.shape, F32)
    gen = jnp.zeros(place.shape, F32)
    for k in range(2 * CAP):
        score = jnp.where(place == k, found[k : k + 1], score)
        gen = jnp.where(place == k, found[2 * CAP + k : 2 * CAP + k + 1], gen)
    masked = jnp.where(live, score, -1e30)
    rank_peak = jnp.max(masked, axis=1, keepdims=True)
    rank_sum = jnp.sum(jnp.where(live, jnp.exp(masked - rank_peak), 0.0), axis=1, keepdims=True)
    rank_norm = rank_peak + jnp.log(rank_sum)
    section = jnp.where(live, score - rank_norm + gen - log_norm + math.log(total_items), 0.0)
    section_ref[...] = section
    chosen = jnp.sum(jnp.where(facts_ref[2:3] > 0.0, section, 0.0), axis=1, keepdims=True)
    weight_ref[...] = chosen + facts_ref[3:4, :128]


def body(
    query, item_table, context_features, candidates, lengths, logged_slot, logging_prop,
    w_first, w_second, w_score,
):
    item_rows, width = item_table.shape
    slots = candidates.shape[1]
    chips = lax.axis_size(CHIPS)
    plane = (lax.axis_size("y"), lax.axis_size("x"), lax.axis_size("z"))
    vmem = pl.BlockSpec(memory_space=pltpu.VMEM)
    smem = pl.BlockSpec(memory_space=pltpu.SMEM)

    message = pl.pallas_call(
        lambda *refs: ask_kernel(plane, chips, item_rows, *refs),
        out_shape=jax.ShapeDtypeStruct((ROWS * chips, 128), BF),
        in_specs=[vmem] * 3,
        out_specs=vmem,
        scratch_shapes=[pltpu.VMEM((ROWS * chips, 128), F32)],
        compiler_params=pltpu.CompilerParams(vmem_limit_bytes=60 * MIB),
        name="ask",
    )(query, context_features, candidates)
    other_table = lax.ppermute(item_table, "core", [(0, 1), (1, 0)])
    asked = lax.all_to_all(
        message.reshape(chips, ROWS, 128), CHIPS, split_axis=0, concat_axis=0, tiled=True
    ).reshape(ROWS * chips, 128)
    facts, chosen = pl.pallas_call(
        lambda *refs: place_kernel(plane, chips, item_rows, *refs),
        out_shape=(
            jax.ShapeDtypeStruct((8, slots), F32),
            jax.ShapeDtypeStruct((chips, slots), BF),
        ),
        in_specs=[vmem] + [smem] * 3,
        out_specs=(vmem, vmem),
        compiler_params=pltpu.CompilerParams(vmem_limit_bytes=8 * MIB),
        cost_estimate=pl.CostEstimate(flops=20000000000, bytes_accessed=600000, transcendentals=0),
        name="place",
    )(candidates, lengths, logged_slot, logging_prop)
    asked, facts = lax.optimization_barrier((asked, facts))
    answers = pl.pallas_call(
        hold_kernel,
        out_shape=jax.ShapeDtypeStruct((chips, 128), F32),
        in_specs=[vmem, vmem, pl.BlockSpec(memory_space=pl.ANY), vmem, vmem, vmem],
        out_specs=vmem,
        scratch_shapes=[
            pltpu.VMEM((ROWS * chips, 128), F32),
            pltpu.VMEM(item_table.shape, BF),
            pltpu.SemaphoreType.DMA,
        ],
        compiler_params=pltpu.CompilerParams(vmem_limit_bytes=51 * MIB),
        name="hold",
    )(asked, item_table, other_table, w_first, w_second, w_score.reshape(1, -1))
    back = lax.all_to_all(
        answers.reshape(chips, 1, 128), CHIPS, split_axis=0, concat_axis=0, tiled=True
    ).reshape(chips, 128)
    total_items = item_rows * 2 * chips
    section, weight = pl.pallas_call(
        lambda *refs: own_kernel(total_items, *refs),
        out_shape=(
            jax.ShapeDtypeStruct((1, slots), F32),
            jax.ShapeDtypeStruct((1, 128), F32),
        ),
        in_specs=[vmem] * 3,
        out_specs=(vmem, vmem),
        compiler_params=pltpu.CompilerParams(vmem_limit_bytes=8 * MIB),
        name="own",
    )(back, chosen, facts)
    return section, weight[0, :1]


def solution(mesh):
    split = Mesh(mesh.devices.reshape(8, 2, 4, 8), ALL)
    row, flat = P(ALL, None), P(ALL)
    placed = (row, row, row, row, flat, flat, flat, P(), P(), P())
    return jax.shard_map(
        body, mesh=split, in_specs=placed, out_specs=(row, flat), check_vma=False
    )
```

```python
import math

import jax
import jax.numpy as jnp
from jax import lax
from jax.experimental import pallas as pl
from jax.experimental.pallas import tpu as pltpu
from jax.sharding import Mesh
from jax.sharding import PartitionSpec as P

ALL = ("y", "core", "x", "z")
CHIPS = ("z", "y", "x")
BIG = float(1 << 24)
CAP = 3
ROWS = 8
MIB = 1 << 20
BF = jnp.bfloat16
F32 = jnp.float32


def dot_nt(a, b):
    return lax.dot_general(a, b, (((1,), (1,)), ((), ())), preferred_element_type=F32)


def dot_nn(a, b):
    return lax.dot_general(a, b, (((1,), (0,)), ((), ())), preferred_element_type=F32)


def silu(v):
    half = 0.5 * v
    return half + half * jnp.tanh(half)


def asked_keys(which, plane, chips, item_rows, ids):
    holder = lax.shift_right_logical(ids, item_rows.bit_length() - 1)
    slot = lax.broadcasted_iota(jnp.int32, ids.shape, 1)
    key = (slot * item_rows + (ids & (item_rows - 1))).astype(F32)
    core = lax.axis_index("core") ^ which
    chip = lax.broadcasted_iota(jnp.int32, (chips, 1), 0)
    rows, columns, depth = plane
    x, y, z = chip % columns, (chip // columns) % rows, chip // (columns * rows)
    device = ((y * 2 + core) * columns + x) * depth + z
    mine = holder == device
    low = jnp.min(jnp.where(mine, key, BIG), axis=1, keepdims=True)
    high = jnp.max(jnp.where(mine, key, -1.0), axis=1, keepdims=True)
    total = jnp.sum(jnp.where(mine, key, 0.0), axis=1, keepdims=True)
    return key, low, high, total


def ask_kernel(plane, chips, item_rows, query_ref, feature_ref, ids_ref, message_ref, spread_ref):
    ids = ids_ref[...]
    lane = lax.broadcasted_iota(jnp.int32, (chips, 128), 1)
    wanted = jnp.full((chips, 128), -1.0, F32)
    for which in range(2):
        _, low, high, total = asked_keys(which, plane, chips, item_rows, ids)
        middle = total - low - high
        least = jnp.where(high >= 0.0, low, -1.0)
        middle = jnp.where((high > low) & (middle > 0.0), middle, -1.0)
        most = jnp.where(high > low, high, -1.0)
        for j, keys in enumerate((least, middle, most)):
            at = 2 * (which * CAP + j)
            wanted = jnp.where((lane == at) | (lane == at + 1), keys, wanted)
    wanted = wanted.astype(jnp.int32)
    inside = jnp.where(wanted < 0, 2 * item_rows, wanted & (item_rows - 1))
    asked = jnp.where((lane & 1) == 0, lax.shift_right_logical(inside, 8), inside & 255)
    asked = asked.astype(F32)
    spread_ref[pl.ds(ROWS - 2, chips, stride=ROWS), :] = asked
    line = lax.broadcasted_iota(jnp.int32, (ROWS, 128), 0)
    own = jnp.zeros((ROWS, 128), F32)
    at = 0
    for ref in (query_ref, feature_ref):
        for k in range(0, ref.shape[1], 128):
            own = jnp.where(line == at, ref[:, k : k + 128].astype(F32), own)
            at += 1
    spread = spread_ref[...].reshape(chips, ROWS, 128)
    spread = jnp.where((line == ROWS - 2)[None], spread, own[None])
    message_ref[...] = spread.reshape(ROWS * chips, 128).astype(BF)


def place_kernel(
    plane, chips, item_rows, ids_ref, length_ref, logged_ref, prop_ref, facts_ref, chosen_ref
):
    ids = ids_ref[...]
    first = jnp.zeros(ids.shape, F32)
    last = jnp.zeros(ids.shape, F32)
    for which in range(2):
        key, low, high, _ = asked_keys(which, plane, chips, item_rows, ids)
        first = first + jnp.sum(jnp.where(low == key, 1.0, 0.0), axis=0, keepdims=True)
        last = last + jnp.sum(jnp.where(high == key, 1.0, 0.0), axis=0, keepdims=True)
    place = jnp.where(first > 0.0, 0, jnp.where(last > 0.0, 2, 1))
    holder = lax.shift_right_logical(ids, item_rows.bit_length() - 1)
    rows, columns, depth = plane
    place = (((holder // (columns * depth)) & 1) ^ lax.axis_index("core")) * CAP + place
    slot = lax.broadcasted_iota(jnp.int32, ids.shape, 1)
    ones = jnp.ones(ids.shape, F32)
    length = length_ref[0]
    facts_ref[0:1] = place.astype(F32)
    facts_ref[1:2] = jnp.where(slot < length, 1.0, 0.0)
    facts_ref[2:3] = jnp.where(slot == logged_ref[0], 1.0, 0.0)
    facts_ref[3:4] = jnp.log(ones * length.astype(F32)) - jnp.log(
        ones * (prop_ref[0].astype(F32) / 1024.0)
    )
    chip_of = (holder % depth) * rows + holder // (2 * columns * depth)
    chip_of = chip_of * columns + (holder // depth) % columns
    chip = lax.broadcasted_iota(jnp.int32, chosen_ref.shape, 0)
    chosen_ref[...] = jnp.where(chip == chip_of, 1.0, 0.0).astype(BF)


def hold_kernel(
    asked_ref, own_ref, other_hbm, w_first_ref, w_second_ref, w_score_ref,
    out_ref, lines_ref, other_ref, other_sem,
):
    half = other_ref.shape[0] // 2
    other_copies = [
        pltpu.make_async_copy(
            other_hbm.at[pl.ds(k * half, half)], other_ref.at[pl.ds(k * half, half)], other_sem.at[k]
        )
        for k in range(2)
    ]
    for copy in other_copies:
        copy.start()
    contexts = asked_ref.shape[0] // ROWS
    tables = (own_ref, other_ref)
    item_rows, width = own_ref.shape
    feature_width = w_first_ref.shape[0] - width
    lines_ref[...] = asked_ref[...].astype(F32)
    lines = [lines_ref[pl.ds(k, contexts, stride=ROWS), :] for k in range(ROWS - 1)]
    query_wide = jnp.concatenate(lines[: width // 128], axis=1)
    query = query_wide.astype(BF)
    features = jnp.concatenate(lines[width // 128 : ROWS - 2], axis=1).astype(BF)
    id_parts = lines[ROWS - 2]
    lane = lax.broadcasted_iota(jnp.int32, (contexts, 128), 1)
    chunk = 1024
    peak = jnp.full((contexts, 128), -1e30, F32)
    total = jnp.zeros((contexts, 128), F32)
    out = jnp.zeros((contexts, 128), F32)
    context_part = dot_nn(features, w_first_ref[:feature_width, :])
    item = lax.broadcasted_iota(jnp.int32, (contexts, item_rows), 1)
    w_score = jnp.broadcast_to(w_score_ref[...], (128, w_score_ref.shape[1]))
    for core in range(2):
        if core == 1:
            for copy in other_copies:
                copy.wait()
        for start in range(0, item_rows, chunk):
            logits = dot_nt(query, tables[core][start : start + chunk, :])
            new = peak
            for k in range(0, chunk, 128):
                new = jnp.maximum(new, logits[:, k : k + 128])
            total = total * jnp.exp(peak - new)
            for k in range(0, chunk, 128):
                total = total + jnp.exp(logits[:, k : k + 128] - new)
            peak = new
        for j in range(CAP):
            place = core * CAP + j
            inside = id_parts[:, 2 * place : 2 * place + 1] * 256.0
            inside = (inside + id_parts[:, 2 * place + 1 : 2 * place + 2]).astype(jnp.int32)
            chosen = jnp.where(item == inside, 1.0, 0.0).astype(BF)
            rows = dot_nn(chosen, tables[core][...])
            gen = jnp.sum(rows * query_wide, axis=1, keepdims=True)
            hidden = silu(dot_nn(rows.astype(BF), w_first_ref[feature_width:, :]) + context_part)
            second = silu(dot_nn(hidden.astype(BF), w_second_ref[...]))
            score = dot_nt(second.astype(BF), w_score)
            out = jnp.where(lane == place, score, out)
            out = jnp.where(lane == 2 * CAP + place, gen, out)
    top = jnp.max(peak, axis=1, keepdims=True)
    total = jnp.sum(total * jnp.exp(peak - top), axis=1, keepdims=True)
    out = jnp.where(lane == 4 * CAP, top, jnp.where(lane == 4 * CAP + 1, total, out))
    out_ref[...] = out


def own_kernel(total_items, back_ref, chosen_ref, facts_ref, section_ref, weight_ref):
    back = jnp.transpose(back_ref[...])[:16]
    top = back.astype(BF)
    rest = back - top.astype(F32)
    middle = rest.astype(BF)
    low = (rest - middle.astype(F32)).astype(BF)
    found = dot_nn(jnp.concatenate([top, middle, low], axis=0), chosen_ref[...])
    found = found[:16] + found[16:32] + found[32:]
    peaks, sums = back[4 * CAP : 4 * CAP + 1], back[4 * CAP + 1 : 4 * CAP + 2]
    peak = jnp.max(peaks, axis=1, keepdims=True)
    log_norm = peak + jnp.log(jnp.sum(sums * jnp.exp(peaks - peak), axis=1, keepdims=True))
    place = facts_ref[0:1]
    live = facts_ref[1:2] > 0.0
    score = jnp.zeros(place.shape, F32)
    gen = jnp.zeros(place.shape, F32)
    for k in range(2 * CAP):
        score = jnp.where(place == k, found[k : k + 1], score)
        gen = jnp.where(place == k, found[2 * CAP + k : 2 * CAP + k + 1], gen)
    masked = jnp.where(live, score, -1e30)
    rank_peak = jnp.max(masked, axis=1, keepdims=True)
    rank_sum = jnp.sum(jnp.where(live, jnp.exp(masked - rank_peak), 0.0), axis=1, keepdims=True)
    rank_norm = rank_peak + jnp.log(rank_sum)
    section = jnp.where(live, score - rank_norm + gen - log_norm + math.log(total_items), 0.0)
    section_ref[...] = section
    chosen = jnp.sum(jnp.where(facts_ref[2:3] > 0.0, section, 0.0), axis=1, keepdims=True)
    weight_ref[...] = chosen + facts_ref[3:4, :128]


def body(
    query, item_table, context_features, candidates, lengths, logged_slot, logging_prop,
    w_first, w_second, w_score,
):
    item_rows, width = item_table.shape
    slots = candidates.shape[1]
    chips = lax.axis_size(CHIPS)
    plane = (lax.axis_size("y"), lax.axis_size("x"), lax.axis_size("z"))
    vmem = pl.BlockSpec(memory_space=pltpu.VMEM)
    smem = pl.BlockSpec(memory_space=pltpu.SMEM)

    message = pl.pallas_call(
        lambda *refs: ask_kernel(plane, chips, item_rows, *refs),
        out_shape=jax.ShapeDtypeStruct((ROWS * chips, 128), BF),
        in_specs=[vmem] * 3,
        out_specs=vmem,
        scratch_shapes=[pltpu.VMEM((ROWS * chips, 128), F32)],
        compiler_params=pltpu.CompilerParams(vmem_limit_bytes=60 * MIB),
        name="ask",
    )(query, context_features, candidates)
    other_table = lax.ppermute(item_table, "core", [(0, 1), (1, 0)])
    asked = lax.all_to_all(
        message.reshape(chips, ROWS, 128), CHIPS, split_axis=0, concat_axis=0, tiled=True
    ).reshape(ROWS * chips, 128)
    facts, chosen = pl.pallas_call(
        lambda *refs: place_kernel(plane, chips, item_rows, *refs),
        out_shape=(
            jax.ShapeDtypeStruct((8, slots), F32),
            jax.ShapeDtypeStruct((chips, slots), BF),
        ),
        in_specs=[vmem] + [smem] * 3,
        out_specs=(vmem, vmem),
        compiler_params=pltpu.CompilerParams(vmem_limit_bytes=8 * MIB),
        cost_estimate=pl.CostEstimate(flops=20000000000, bytes_accessed=600000, transcendentals=0),
        name="place",
    )(candidates, lengths, logged_slot, logging_prop)
    asked, facts = lax.optimization_barrier((asked, facts))
    answers = pl.pallas_call(
        hold_kernel,
        out_shape=jax.ShapeDtypeStruct((chips, 128), F32),
        in_specs=[vmem, vmem, pl.BlockSpec(memory_space=pl.ANY), vmem, vmem, vmem],
        out_specs=vmem,
        scratch_shapes=[
            pltpu.VMEM((ROWS * chips, 128), F32),
            pltpu.VMEM(item_table.shape, BF),
            pltpu.SemaphoreType.DMA((2,)),
        ],
        compiler_params=pltpu.CompilerParams(vmem_limit_bytes=51 * MIB),
        name="hold",
    )(asked, item_table, other_table, w_first, w_second, w_score.reshape(1, -1))
    back = lax.all_to_all(
        answers.reshape(chips, 1, 128), CHIPS, split_axis=0, concat_axis=0, tiled=True
    ).reshape(chips, 128)
    total_items = item_rows * 2 * chips
    section, weight = pl.pallas_call(
        lambda *refs: own_kernel(total_items, *refs),
        out_shape=(
            jax.ShapeDtypeStruct((1, slots), F32),
            jax.ShapeDtypeStruct((1, 128), F32),
        ),
        in_specs=[vmem] * 3,
        out_specs=(vmem, vmem),
        compiler_params=pltpu.CompilerParams(vmem_limit_bytes=8 * MIB),
        name="own",
    )(back, chosen, facts)
    return section, weight[0, :1]


def solution(mesh):
    split = Mesh(mesh.devices.reshape(8, 2, 4, 8), ALL)
    row, flat = P(ALL, None), P(ALL)
    placed = (row, row, row, row, flat, flat, flat, P(), P(), P())
    return jax.shard_map(
        body, mesh=split, in_specs=placed, out_specs=(row, flat), check_vma=False
    )
```

```python
import math

import jax
import jax.numpy as jnp
from jax import lax
from jax.experimental import pallas as pl
from jax.experimental.pallas import tpu as pltpu
from jax.sharding import Mesh
from jax.sharding import PartitionSpec as P

ALL = ("y", "core", "x", "z")
CHIPS = ("z", "y", "x")
BIG = float(1 << 24)
CAP = 3
ROWS = 8
MIB = 1 << 20
BF = jnp.bfloat16
F32 = jnp.float32


def dot_nt(a, b):
    return lax.dot_general(a, b, (((1,), (1,)), ((), ())), preferred_element_type=F32)


def dot_nn(a, b):
    return lax.dot_general(a, b, (((1,), (0,)), ((), ())), preferred_element_type=F32)


def silu(v):
    half = 0.5 * v
    return half + half * jnp.tanh(half)


def asked_keys(which, plane, chips, item_rows, ids):
    holder = lax.shift_right_logical(ids, item_rows.bit_length() - 1)
    slot = lax.broadcasted_iota(jnp.int32, ids.shape, 1)
    key = (slot * item_rows + (ids & (item_rows - 1))).astype(F32)
    core = lax.axis_index("core") ^ which
    chip = lax.broadcasted_iota(jnp.int32, (chips, 1), 0)
    rows, columns, depth = plane
    x, y, z = chip % columns, (chip // columns) % rows, chip // (columns * rows)
    device = ((y * 2 + core) * columns + x) * depth + z
    mine = holder == device
    low = jnp.min(jnp.where(mine, key, BIG), axis=1, keepdims=True)
    high = jnp.max(jnp.where(mine, key, -1.0), axis=1, keepdims=True)
    total = jnp.sum(jnp.where(mine, key, 0.0), axis=1, keepdims=True)
    return key, low, high, total


def ask_kernel(plane, chips, item_rows, query_ref, feature_ref, ids_ref, message_ref, spread_ref):
    ids = ids_ref[...]
    lane = lax.broadcasted_iota(jnp.int32, (chips, 128), 1)
    wanted = jnp.full((chips, 128), -1.0, F32)
    for which in range(2):
        _, low, high, total = asked_keys(which, plane, chips, item_rows, ids)
        middle = total - low - high
        least = jnp.where(high >= 0.0, low, -1.0)
        middle = jnp.where((high > low) & (middle > 0.0), middle, -1.0)
        most = jnp.where(high > low, high, -1.0)
        for j, keys in enumerate((least, middle, most)):
            at = 2 * (which * CAP + j)
            wanted = jnp.where((lane == at) | (lane == at + 1), keys, wanted)
    wanted = wanted.astype(jnp.int32)
    inside = jnp.where(wanted < 0, 2 * item_rows, wanted & (item_rows - 1))
    asked = jnp.where((lane & 1) == 0, lax.shift_right_logical(inside, 8), inside & 255)
    asked = asked.astype(F32)
    spread_ref[pl.ds(ROWS - 2, chips, stride=ROWS), :] = asked
    line = lax.broadcasted_iota(jnp.int32, (ROWS, 128), 0)
    own = jnp.zeros((ROWS, 128), F32)
    at = 0
    for ref in (query_ref, feature_ref):
        for k in range(0, ref.shape[1], 128):
            own = jnp.where(line == at, ref[:, k : k + 128].astype(F32), own)
            at += 1
    spread = spread_ref[...].reshape(chips, ROWS, 128)
    spread = jnp.where((line == ROWS - 2)[None], spread, own[None])
    message_ref[...] = spread.reshape(ROWS * chips, 128).astype(BF)


def place_kernel(
    plane, chips, item_rows, ids_ref, length_ref, logged_ref, prop_ref, facts_ref, chosen_ref
):
    ids = ids_ref[...]
    first = jnp.zeros(ids.shape, F32)
    last = jnp.zeros(ids.shape, F32)
    for which in range(2):
        key, low, high, _ = asked_keys(which, plane, chips, item_rows, ids)
        first = first + jnp.sum(jnp.where(low == key, 1.0, 0.0), axis=0, keepdims=True)
        last = last + jnp.sum(jnp.where(high == key, 1.0, 0.0), axis=0, keepdims=True)
    place = jnp.where(first > 0.0, 0, jnp.where(last > 0.0, 2, 1))
    holder = lax.shift_right_logical(ids, item_rows.bit_length() - 1)
    rows, columns, depth = plane
    place = (((holder // (columns * depth)) & 1) ^ lax.axis_index("core")) * CAP + place
    slot = lax.broadcasted_iota(jnp.int32, ids.shape, 1)
    ones = jnp.ones(ids.shape, F32)
    length = length_ref[0]
    facts_ref[0:1] = place.astype(F32)
    facts_ref[1:2] = jnp.where(slot < length, 1.0, 0.0)
    facts_ref[2:3] = jnp.where(slot == logged_ref[0], 1.0, 0.0)
    facts_ref[3:4] = jnp.log(ones * length.astype(F32)) - jnp.log(
        ones * (prop_ref[0].astype(F32) / 1024.0)
    )
    chip_of = (holder % depth) * rows + holder // (2 * columns * depth)
    chip_of = chip_of * columns + (holder // depth) % columns
    chip = lax.broadcasted_iota(jnp.int32, chosen_ref.shape, 0)
    chosen_ref[...] = jnp.where(chip == chip_of, 1.0, 0.0).astype(BF)


def hold_kernel(
    asked_ref, own_ref, other_hbm, w_first_ref, w_second_ref, w_score_ref,
    out_ref, lines_ref, other_ref, other_sem,
):
    other_copy = pltpu.make_async_copy(other_hbm, other_ref, other_sem)
    other_copy.start()
    contexts = asked_ref.shape[0] // ROWS
    tables = (own_ref, other_ref)
    item_rows, width = own_ref.shape
    feature_width = w_first_ref.shape[0] - width
    lines_ref[...] = asked_ref[...].astype(F32)
    lines = [lines_ref[pl.ds(k, contexts, stride=ROWS), :] for k in range(ROWS - 1)]
    query_wide = jnp.concatenate(lines[: width // 128], axis=1)
    query = query_wide.astype(BF)
    features = jnp.concatenate(lines[width // 128 : ROWS - 2], axis=1).astype(BF)
    id_parts = lines[ROWS - 2]
    lane = lax.broadcasted_iota(jnp.int32, (contexts, 128), 1)
    chunk = 1024
    peak = jnp.full((contexts, 128), -1e30, F32)
    total = jnp.zeros((contexts, 128), F32)
    out = jnp.zeros((contexts, 128), F32)
    context_part = dot_nn(features, w_first_ref[:feature_width, :])
    item = lax.broadcasted_iota(jnp.int32, (contexts, item_rows), 1)
    w_score = jnp.broadcast_to(w_score_ref[...], (128, w_score_ref.shape[1]))
    for core in range(2):
        if core == 1:
            other_copy.wait()
        for start in range(0, item_rows, chunk):
            logits = dot_nt(query, tables[core][start : start + chunk, :])
            new = peak
            for k in range(0, chunk, 128):
                new = jnp.maximum(new, logits[:, k : k + 128])
            total = total * jnp.exp(peak - new)
            for k in range(0, chunk, 128):
                total = total + jnp.exp(logits[:, k : k + 128] - new)
            peak = new
        found = []
        for j in range(CAP):
            place = core * CAP + j
            inside = id_parts[:, 2 * place : 2 * place + 1] * 256.0
            inside = (inside + id_parts[:, 2 * place + 1 : 2 * place + 2]).astype(jnp.int32)
            chosen = jnp.where(item == inside, 1.0, 0.0).astype(BF)
            rows = dot_nn(chosen, tables[core][...])
            gen = jnp.sum(rows * query_wide, axis=1, keepdims=True)
            out = jnp.where(lane == 2 * CAP + place, gen, out)
            found.append(rows.astype(BF))
        for j in range(CAP):
            hidden = silu(dot_nn(found[j], w_first_ref[feature_width:, :]) + context_part)
            second = silu(dot_nn(hidden.astype(BF), w_second_ref[...]))
            score = dot_nt(second.astype(BF), w_score)
            out = jnp.where(lane == core * CAP + j, score, out)
    top = jnp.max(peak, axis=1, keepdims=True)
    total = jnp.sum(total * jnp.exp(peak - top), axis=1, keepdims=True)
    out = jnp.where(lane == 4 * CAP, top, jnp.where(lane == 4 * CAP + 1, total, out))
    out_ref[...] = out


def own_kernel(total_items, back_ref, chosen_ref, facts_ref, section_ref, weight_ref):
    back = jnp.transpose(back_ref[...])[:16]
    top = back.astype(BF)
    rest = back - top.astype(F32)
    middle = rest.astype(BF)
    low = (rest - middle.astype(F32)).astype(BF)
    found = dot_nn(jnp.concatenate([top, middle, low], axis=0), chosen_ref[...])
    found = found[:16] + found[16:32] + found[32:]
    peaks, sums = back[4 * CAP : 4 * CAP + 1], back[4 * CAP + 1 : 4 * CAP + 2]
    peak = jnp.max(peaks, axis=1, keepdims=True)
    log_norm = peak + jnp.log(jnp.sum(sums * jnp.exp(peaks - peak), axis=1, keepdims=True))
    place = facts_ref[0:1]
    live = facts_ref[1:2] > 0.0
    score = jnp.zeros(place.shape, F32)
    gen = jnp.zeros(place.shape, F32)
    for k in range(2 * CAP):
        score = jnp.where(place == k, found[k : k + 1], score)
        gen = jnp.where(place == k, found[2 * CAP + k : 2 * CAP + k + 1], gen)
    masked = jnp.where(live, score, -1e30)
    rank_peak = jnp.max(masked, axis=1, keepdims=True)
    rank_sum = jnp.sum(jnp.where(live, jnp.exp(masked - rank_peak), 0.0), axis=1, keepdims=True)
    rank_norm = rank_peak + jnp.log(rank_sum)
    section = jnp.where(live, score - rank_norm + gen - log_norm + math.log(total_items), 0.0)
    section_ref[...] = section
    chosen = jnp.sum(jnp.where(facts_ref[2:3] > 0.0, section, 0.0), axis=1, keepdims=True)
    weight_ref[...] = chosen + facts_ref[3:4, :128]


def body(
    query, item_table, context_features, candidates, lengths, logged_slot, logging_prop,
    w_first, w_second, w_score,
):
    item_rows, width = item_table.shape
    slots = candidates.shape[1]
    chips = lax.axis_size(CHIPS)
    plane = (lax.axis_size("y"), lax.axis_size("x"), lax.axis_size("z"))
    vmem = pl.BlockSpec(memory_space=pltpu.VMEM)
    smem = pl.BlockSpec(memory_space=pltpu.SMEM)

    message = pl.pallas_call(
        lambda *refs: ask_kernel(plane, chips, item_rows, *refs),
        out_shape=jax.ShapeDtypeStruct((ROWS * chips, 128), BF),
        in_specs=[vmem] * 3,
        out_specs=vmem,
        scratch_shapes=[pltpu.VMEM((ROWS * chips, 128), F32)],
        compiler_params=pltpu.CompilerParams(vmem_limit_bytes=60 * MIB),
        name="ask",
    )(query, context_features, candidates)
    other_table = lax.ppermute(item_table, "core", [(0, 1), (1, 0)])
    asked = lax.all_to_all(
        message.reshape(chips, ROWS, 128), CHIPS, split_axis=0, concat_axis=0, tiled=True
    ).reshape(ROWS * chips, 128)
    facts, chosen = pl.pallas_call(
        lambda *refs: place_kernel(plane, chips, item_rows, *refs),
        out_shape=(
            jax.ShapeDtypeStruct((8, slots), F32),
            jax.ShapeDtypeStruct((chips, slots), BF),
        ),
        in_specs=[vmem] + [smem] * 3,
        out_specs=(vmem, vmem),
        compiler_params=pltpu.CompilerParams(vmem_limit_bytes=8 * MIB),
        cost_estimate=pl.CostEstimate(flops=20000000000, bytes_accessed=600000, transcendentals=0),
        name="place",
    )(candidates, lengths, logged_slot, logging_prop)
    asked, facts = lax.optimization_barrier((asked, facts))
    answers = pl.pallas_call(
        hold_kernel,
        out_shape=jax.ShapeDtypeStruct((chips, 128), F32),
        in_specs=[vmem, vmem, pl.BlockSpec(memory_space=pl.ANY), vmem, vmem, vmem],
        out_specs=vmem,
        scratch_shapes=[
            pltpu.VMEM((ROWS * chips, 128), F32),
            pltpu.VMEM(item_table.shape, BF),
            pltpu.SemaphoreType.DMA,
        ],
        compiler_params=pltpu.CompilerParams(vmem_limit_bytes=51 * MIB),
        name="hold",
    )(asked, item_table, other_table, w_first, w_second, w_score.reshape(1, -1))
    back = lax.all_to_all(
        answers.reshape(chips, 1, 128), CHIPS, split_axis=0, concat_axis=0, tiled=True
    ).reshape(chips, 128)
    total_items = item_rows * 2 * chips
    section, weight = pl.pallas_call(
        lambda *refs: own_kernel(total_items, *refs),
        out_shape=(
            jax.ShapeDtypeStruct((1, slots), F32),
            jax.ShapeDtypeStruct((1, 128), F32),
        ),
        in_specs=[vmem] * 3,
        out_specs=(vmem, vmem),
        compiler_params=pltpu.CompilerParams(vmem_limit_bytes=8 * MIB),
        name="own",
    )(back, chosen, facts)
    return section, weight[0, :1]


def solution(mesh):
    split = Mesh(mesh.devices.reshape(8, 2, 4, 8), ALL)
    row, flat = P(ALL, None), P(ALL)
    placed = (row, row, row, row, flat, flat, flat, P(), P(), P())
    return jax.shard_map(
        body, mesh=split, in_specs=placed, out_specs=(row, flat), check_vma=False
    )
```

```python
import math

import jax
import jax.numpy as jnp
from jax import lax
from jax.experimental import pallas as pl
from jax.experimental.pallas import tpu as pltpu
from jax.sharding import Mesh
from jax.sharding import PartitionSpec as P

ALL = ("y", "core", "x", "z")
CHIPS = ("z", "y", "x")
BIG = float(1 << 24)
CAP = 3
ROWS = 8
MIB = 1 << 20
BF = jnp.bfloat16
F32 = jnp.float32


def dot_nt(a, b):
    return lax.dot_general(a, b, (((1,), (1,)), ((), ())), preferred_element_type=F32)


def dot_nn(a, b):
    return lax.dot_general(a, b, (((1,), (0,)), ((), ())), preferred_element_type=F32)


def silu(v):
    half = 0.5 * v
    return half + half * jnp.tanh(half)


def asked_keys(which, plane, chips, item_rows, ids):
    holder = lax.shift_right_logical(ids, item_rows.bit_length() - 1)
    slot = lax.broadcasted_iota(jnp.int32, ids.shape, 1)
    key = (slot * item_rows + (ids & (item_rows - 1))).astype(F32)
    core = lax.axis_index("core") ^ which
    chip = lax.broadcasted_iota(jnp.int32, (chips, 1), 0)
    rows, columns, depth = plane
    x, y, z = chip % columns, (chip // columns) % rows, chip // (columns * rows)
    device = ((y * 2 + core) * columns + x) * depth + z
    mine = holder == device
    low = jnp.min(jnp.where(mine, key, BIG), axis=1, keepdims=True)
    high = jnp.max(jnp.where(mine, key, -1.0), axis=1, keepdims=True)
    total = jnp.sum(jnp.where(mine, key, 0.0), axis=1, keepdims=True)
    return key, low, high, total


def ask_kernel(plane, chips, item_rows, query_ref, feature_ref, ids_ref, message_ref, spread_ref):
    ids = ids_ref[...]
    lane = lax.broadcasted_iota(jnp.int32, (chips, 128), 1)
    wanted = jnp.full((chips, 128), -1.0, F32)
    for which in range(2):
        _, low, high, total = asked_keys(which, plane, chips, item_rows, ids)
        middle = total - low - high
        least = jnp.where(high >= 0.0, low, -1.0)
        middle = jnp.where((high > low) & (middle > 0.0), middle, -1.0)
        most = jnp.where(high > low, high, -1.0)
        for j, keys in enumerate((least, middle, most)):
            at = 2 * (which * CAP + j)
            wanted = jnp.where((lane == at) | (lane == at + 1), keys, wanted)
    wanted = wanted.astype(jnp.int32)
    inside = jnp.where(wanted < 0, 2 * item_rows, wanted & (item_rows - 1))
    asked = jnp.where((lane & 1) == 0, lax.shift_right_logical(inside, 8), inside & 255)
    asked = asked.astype(F32)
    spread_ref[pl.ds(ROWS - 2, chips, stride=ROWS), :] = asked
    line = lax.broadcasted_iota(jnp.int32, (ROWS, 128), 0)
    own = jnp.zeros((ROWS, 128), F32)
    at = 0
    for ref in (query_ref, feature_ref):
        for k in range(0, ref.shape[1], 128):
            own = jnp.where(line == at, ref[:, k : k + 128].astype(F32), own)
            at += 1
    spread = spread_ref[...].reshape(chips, ROWS, 128)
    spread = jnp.where((line == ROWS - 2)[None], spread, own[None])
    message_ref[...] = spread.reshape(ROWS * chips, 128).astype(BF)


def place_kernel(
    plane, chips, item_rows, ids_ref, length_ref, logged_ref, prop_ref, facts_ref, chosen_ref
):
    ids = ids_ref[...]
    first = jnp.zeros(ids.shape, F32)
    last = jnp.zeros(ids.shape, F32)
    for which in range(2):
        key, low, high, _ = asked_keys(which, plane, chips, item_rows, ids)
        first = first + jnp.sum(jnp.where(low == key, 1.0, 0.0), axis=0, keepdims=True)
        last = last + jnp.sum(jnp.where(high == key, 1.0, 0.0), axis=0, keepdims=True)
    place = jnp.where(first > 0.0, 0, jnp.where(last > 0.0, 2, 1))
    holder = lax.shift_right_logical(ids, item_rows.bit_length() - 1)
    rows, columns, depth = plane
    place = (((holder // (columns * depth)) & 1) ^ lax.axis_index("core")) * CAP + place
    slot = lax.broadcasted_iota(jnp.int32, ids.shape, 1)
    ones = jnp.ones(ids.shape, F32)
    length = length_ref[0]
    facts_ref[0:1] = place.astype(F32)
    facts_ref[1:2] = jnp.where(slot < length, 1.0, 0.0)
    facts_ref[2:3] = jnp.where(slot == logged_ref[0], 1.0, 0.0)
    facts_ref[3:4] = jnp.log(ones * length.astype(F32)) - jnp.log(
        ones * (prop_ref[0].astype(F32) / 1024.0)
    )
    chip_of = (holder % depth) * rows + holder // (2 * columns * depth)
    chip_of = chip_of * columns + (holder // depth) % columns
    chip = lax.broadcasted_iota(jnp.int32, chosen_ref.shape, 0)
    chosen_ref[...] = jnp.where(chip == chip_of, 1.0, 0.0).astype(BF)


def hold_kernel(
    asked_ref, own_ref, other_hbm, w_first_ref, w_second_ref, w_score_ref,
    out_ref, lines_ref, other_ref, other_sem,
):
    other_copy = pltpu.make_async_copy(other_hbm, other_ref, other_sem)
    other_copy.start()
    contexts = asked_ref.shape[0] // ROWS
    tables = (own_ref, other_ref)
    item_rows, width = own_ref.shape
    feature_width = w_first_ref.shape[0] - width
    lines_ref[...] = asked_ref[...].astype(F32)
    lines = [lines_ref[pl.ds(k, contexts, stride=ROWS), :] for k in range(ROWS - 1)]
    query_wide = jnp.concatenate(lines[: width // 128], axis=1)
    query = query_wide.astype(BF)
    features = jnp.concatenate(lines[width // 128 : ROWS - 2], axis=1).astype(BF)
    id_parts = lines[ROWS - 2]
    lane = lax.broadcasted_iota(jnp.int32, (contexts, 128), 1)
    chunk = 1024
    peak = jnp.full((contexts, 128), -1e30, F32)
    total = jnp.zeros((contexts, 128), F32)
    out = jnp.zeros((contexts, 128), F32)
    context_part = dot_nn(features, w_first_ref[:feature_width, :])
    item = lax.broadcasted_iota(jnp.int32, (contexts, item_rows), 1)
    w_score = jnp.broadcast_to(w_score_ref[...], (128, w_score_ref.shape[1]))
    for core in range(2):
        if core == 1:
            other_copy.wait()
        for start in range(0, item_rows, chunk):
            logits = dot_nt(query, tables[core][start : start + chunk, :])
            new = peak
            for k in range(0, chunk, 128):
                new = jnp.maximum(new, logits[:, k : k + 128])
            total = total * jnp.exp(peak - new)
            for k in range(0, chunk, 128):
                total = total + jnp.exp(logits[:, k : k + 128] - new)
            peak = new
        found = []
        for j in range(CAP):
            place = core * CAP + j
            inside = id_parts[:, 2 * place : 2 * place + 1] * 256.0
            inside = (inside + id_parts[:, 2 * place + 1 : 2 * place + 2]).astype(jnp.int32)
            chosen = jnp.where(item == inside, 1.0, 0.0).astype(BF)
            rows = dot_nn(chosen, tables[core][...])
            gen = jnp.sum(rows * query_wide, axis=1, keepdims=True)
            out = jnp.where(lane == 2 * CAP + place, gen, out)
            found.append(rows.astype(BF))
        for j in range(CAP):
            hidden = silu(dot_nn(found[j], w_first_ref[feature_width:, :]) + context_part)
            found[j] = hidden.astype(BF)
        for j in range(CAP):
            second = silu(dot_nn(found[j], w_second_ref[...]))
            score = dot_nt(second.astype(BF), w_score)
            out = jnp.where(lane == core * CAP + j, score, out)
    top = jnp.max(peak, axis=1, keepdims=True)
    total = jnp.sum(total * jnp.exp(peak - top), axis=1, keepdims=True)
    out = jnp.where(lane == 4 * CAP, top, jnp.where(lane == 4 * CAP + 1, total, out))
    out_ref[...] = out


def own_kernel(total_items, back_ref, chosen_ref, facts_ref, section_ref, weight_ref):
    back = jnp.transpose(back_ref[...])[:16]
    top = back.astype(BF)
    rest = back - top.astype(F32)
    middle = rest.astype(BF)
    low = (rest - middle.astype(F32)).astype(BF)
    found = dot_nn(jnp.concatenate([top, middle, low], axis=0), chosen_ref[...])
    found = found[:16] + found[16:32] + found[32:]
    peaks, sums = back[4 * CAP : 4 * CAP + 1], back[4 * CAP + 1 : 4 * CAP + 2]
    peak = jnp.max(peaks, axis=1, keepdims=True)
    log_norm = peak + jnp.log(jnp.sum(sums * jnp.exp(peaks - peak), axis=1, keepdims=True))
    place = facts_ref[0:1]
    live = facts_ref[1:2] > 0.0
    score = jnp.zeros(place.shape, F32)
    gen = jnp.zeros(place.shape, F32)
    for k in range(2 * CAP):
        score = jnp.where(place == k, found[k : k + 1], score)
        gen = jnp.where(place == k, found[2 * CAP + k : 2 * CAP + k + 1], gen)
    masked = jnp.where(live, score, -1e30)
    rank_peak = jnp.max(masked, axis=1, keepdims=True)
    rank_sum = jnp.sum(jnp.where(live, jnp.exp(masked - rank_peak), 0.0), axis=1, keepdims=True)
    rank_norm = rank_peak + jnp.log(rank_sum)
    section = jnp.where(live, score - rank_norm + gen - log_norm + math.log(total_items), 0.0)
    section_ref[...] = section
    chosen = jnp.sum(jnp.where(facts_ref[2:3] > 0.0, section, 0.0), axis=1, keepdims=True)
    weight_ref[...] = chosen + facts_ref[3:4, :128]


def body(
    query, item_table, context_features, candidates, lengths, logged_slot, logging_prop,
    w_first, w_second, w_score,
):
    item_rows, width = item_table.shape
    slots = candidates.shape[1]
    chips = lax.axis_size(CHIPS)
    plane = (lax.axis_size("y"), lax.axis_size("x"), lax.axis_size("z"))
    vmem = pl.BlockSpec(memory_space=pltpu.VMEM)
    smem = pl.BlockSpec(memory_space=pltpu.SMEM)

    message = pl.pallas_call(
        lambda *refs: ask_kernel(plane, chips, item_rows, *refs),
        out_shape=jax.ShapeDtypeStruct((ROWS * chips, 128), BF),
        in_specs=[vmem] * 3,
        out_specs=vmem,
        scratch_shapes=[pltpu.VMEM((ROWS * chips, 128), F32)],
        compiler_params=pltpu.CompilerParams(vmem_limit_bytes=60 * MIB),
        name="ask",
    )(query, context_features, candidates)
    other_table = lax.ppermute(item_table, "core", [(0, 1), (1, 0)])
    asked = lax.all_to_all(
        message.reshape(chips, ROWS, 128), CHIPS, split_axis=0, concat_axis=0, tiled=True
    ).reshape(ROWS * chips, 128)
    facts, chosen = pl.pallas_call(
        lambda *refs: place_kernel(plane, chips, item_rows, *refs),
        out_shape=(
            jax.ShapeDtypeStruct((8, slots), F32),
            jax.ShapeDtypeStruct((chips, slots), BF),
        ),
        in_specs=[vmem] + [smem] * 3,
        out_specs=(vmem, vmem),
        compiler_params=pltpu.CompilerParams(vmem_limit_bytes=8 * MIB),
        cost_estimate=pl.CostEstimate(flops=20000000000, bytes_accessed=600000, transcendentals=0),
        name="place",
    )(candidates, lengths, logged_slot, logging_prop)
    asked, facts = lax.optimization_barrier((asked, facts))
    answers = pl.pallas_call(
        hold_kernel,
        out_shape=jax.ShapeDtypeStruct((chips, 128), F32),
        in_specs=[vmem, vmem, pl.BlockSpec(memory_space=pl.ANY), vmem, vmem, vmem],
        out_specs=vmem,
        scratch_shapes=[
            pltpu.VMEM((ROWS * chips, 128), F32),
            pltpu.VMEM(item_table.shape, BF),
            pltpu.SemaphoreType.DMA,
        ],
        compiler_params=pltpu.CompilerParams(vmem_limit_bytes=51 * MIB),
        name="hold",
    )(asked, item_table, other_table, w_first, w_second, w_score.reshape(1, -1))
    back = lax.all_to_all(
        answers.reshape(chips, 1, 128), CHIPS, split_axis=0, concat_axis=0, tiled=True
    ).reshape(chips, 128)
    total_items = item_rows * 2 * chips
    section, weight = pl.pallas_call(
        lambda *refs: own_kernel(total_items, *refs),
        out_shape=(
            jax.ShapeDtypeStruct((1, slots), F32),
            jax.ShapeDtypeStruct((1, 128), F32),
        ),
        in_specs=[vmem] * 3,
        out_specs=(vmem, vmem),
        compiler_params=pltpu.CompilerParams(vmem_limit_bytes=8 * MIB),
        name="own",
    )(back, chosen, facts)
    return section, weight[0, :1]


def solution(mesh):
    split = Mesh(mesh.devices.reshape(8, 2, 4, 8), ALL)
    row, flat = P(ALL, None), P(ALL)
    placed = (row, row, row, row, flat, flat, flat, P(), P(), P())
    return jax.shard_map(
        body, mesh=split, in_specs=placed, out_specs=(row, flat), check_vma=False
    )
```
